512 devices in a mesh: dp: 32 (over y, x, core), tensor: 16 (over z).
Axes of the slice: x: 4, y: 4, z: 16, core: 2. Of those that a mesh axis runs over, the one named last changes fastest.
Arguments:
- activations: bfloat16 [32768, 5120], P('dp', 'tensor'), may hold values from -36 to 36, as said below
- out_grads: bfloat16 [32768, 4096], P('dp', 'tensor'), may hold values from -0.04375 to 0.04375, as said below
Outputs:
- combined: float32 [5120, 4096], P('dp', 'tensor')
The draws below stay inside these ranges and needn't reach their ends.
Inputs may be any that keep to these rules, and one draw needn't show every extreme that they name: Replicas' activations share a common part and features have different scales. `out_grads`: Replicas' output gradients share a common part and columns have different scales.
All inputs are finite; a program needn't handle non-finite values.
Results may differ from the reference program's by a relative error of at most 0.0003.
Values may be sent and summed in bfloat16 or wider, within the bound.
No kernel may reach another device: no remote copies, remote signals or barrier semaphores. Data moves between devices by JAX's collectives and lax.ppermute only.
A program may use at most 64 MiB of HBM per device.

```python
import math
import jax
import jax.numpy as jnp

D = 5120
F = 4096
TOK_DEV = 1024
REPLICAS = 32


def assemble(common_part, own_part, common_weight, own_weight, top_scale, feature_scale, overall):
    ladder = 1.0 + (top_scale - 1.0) * jnp.arange(REPLICAS, dtype=jnp.float32) / max(REPLICAS - 1, 1)
    mixed = common_weight * common_part[None] + own_weight * own_part
    mixed = mixed * ladder[:, None, None] * feature_scale[None, None, :] * overall
    return mixed.reshape(REPLICAS * common_part.shape[0], common_part.shape[1])


def draw_activations(key, part):
    key = jax.random.fold_in(key, 11)
    key_common, key_own, key_scale = jax.random.split(key, 3)
    feature_scale = jnp.exp(jax.random.uniform(key_scale, (D,), jnp.float32, -0.5 * math.log(10.0), 0.5 * math.log(10.0)))
    common_part = jax.random.normal(key_common, (TOK_DEV, D), jnp.float32)
    own_part = jax.random.normal(key_own, (REPLICAS, TOK_DEV, D), jnp.float32)
    result = assemble(common_part, own_part, 0.8, 0.6, 3.0, feature_scale, 1.0)
    return jnp.clip(result, -36.0, 36.0).astype(jnp.bfloat16)


def draw_out_grads(key, part):
    key = jax.random.fold_in(key, 23)
    key_common, key_own, key_scale = jax.random.split(key, 3)
    feature_scale = jnp.exp(jax.random.uniform(key_scale, (F,), jnp.float32, -0.5 * math.log(10.0), 0.5 * math.log(10.0)))
    overall = 0.2 / math.sqrt(TOK_DEV)
    limit = 1.4 / math.sqrt(TOK_DEV)
    common_part = jax.random.normal(key_common, (TOK_DEV, F), jnp.float32)
    own_part = jax.random.normal(key_own, (REPLICAS, TOK_DEV, F), jnp.float32)
    result = assemble(common_part, own_part, 0.8, 0.6, 1.0, feature_scale, overall)
    return jnp.clip(result, -limit, limit).astype(jnp.bfloat16)


def setup_inputs(seed: int = 0) -> dict:
    key_list = jax.random.split(jax.random.key(seed), 3)
    activations = draw_activations(jax.random.fold_in(key_list[2], 71), 0)
    out_grads = draw_out_grads(jax.random.fold_in(key_list[2], 71), 0)
    return dict(activations=activations, out_grads=out_grads)


epsilon = 1e-06

def adasum(left, right):
    cross_dot = jnp.sum(left * right)
    left_norm = jnp.sum(left * left)
    right_norm = jnp.sum(right * right)
    return (1.0 - cross_dot / (2.0 * (left_norm + epsilon))) * left + (1.0 - cross_dot / (2.0 * (right_norm + epsilon))) * right

def reference(activations, out_grads):

    def replica_grad(replica_index):
        rows_x = activations[replica_index * TOK_DEV:(replica_index + 1) * TOK_DEV]
        grad_rows = out_grads[replica_index * TOK_DEV:(replica_index + 1) * TOK_DEV]
        return jnp.dot(rows_x.T, grad_rows, preferred_element_type=jnp.float32)

    def combined_tree(lower_index, members):
        if members == 1:
            return replica_grad(lower_index)
        half_count = members // 2
        return adasum(combined_tree(lower_index, half_count), combined_tree(lower_index + half_count, half_count))
    return combined_tree(0, REPLICAS)
```

```python
import jax
import jax.numpy as jnp
from jax import lax
from jax.sharding import PartitionSpec as P

epsilon = 1e-06
CHUNKS = 1


def gram_total(gram):
    n = gram.shape[0]
    flat = gram.reshape(-1, 128)
    flat = jnp.sum(lax.all_gather(flat, "dp"), axis=0)
    peers = jnp.broadcast_to(flat, (lax.axis_size("tensor"), *flat.shape))
    flat = jnp.sum(lax.all_to_all(peers, "tensor", 0, 0), axis=0)
    return flat.reshape(n, n)


def tree_weights(gram):
    n = gram.shape[0]
    index = jnp.arange(n)
    weights = jnp.ones((n,), jnp.float32)
    width = 1
    while width < n:
        scaled = gram * weights[:, None] * weights[None, :]
        item = index // width
        same = (item[:, None] == item[None, :])
        partner = (item[:, None] == (item ^ 1)[None, :])
        own = jnp.sum(jnp.where(same, scaled, 0.0), axis=1)
        cross = jnp.sum(jnp.where(partner, scaled, 0.0), axis=1)
        own = jnp.sum(jnp.where(same, own[None, :], 0.0), axis=1)
        cross = jnp.sum(jnp.where(same, cross[None, :], 0.0), axis=1)
        own = jnp.maximum(own, 0.0)
        weights = weights * (1.0 - cross / (2.0 * (own + epsilon)))
        width *= 2
    return weights


def on_device(activations, out_grads):
    replicas = lax.axis_size("dp")
    slabs = lax.axis_size("tensor")
    tokens, slab_rows = activations.shape
    columns = out_grads.shape[1]
    block_rows = slab_rows * slabs // replicas
    per_slab = slab_rows // block_rows
    rows = block_rows // CHUNKS
    x = activations.T.reshape(per_slab, CHUNKS, rows, tokens)
    blocks = []
    gram = jnp.zeros((replicas, replicas), jnp.float32)
    for chunk in range(CHUNKS):
        part = lax.all_gather(x[:, chunk], "tensor", axis=0)
        part = part.reshape(replicas * rows, tokens)
        grad = jnp.dot(part, out_grads, preferred_element_type=jnp.float32)
        grad = grad.reshape(replicas, rows, columns)
        block = lax.all_to_all(grad, "dp", 0, 0)
        blocks.append(block)
        gram = gram + lax.dot_general(
            block, block, (((1, 2), (1, 2)), ((), ())),
            precision=lax.Precision.HIGHEST, preferred_element_type=jnp.float32,
        )
    weights = tree_weights(gram_total(gram))
    out = [jnp.sum(b * weights[:, None, None], axis=0) for b in blocks]
    return jnp.concatenate(out, axis=0)


def solution(mesh):
    return jax.shard_map(
        on_device,
        mesh=mesh,
        in_specs=(P("dp", "tensor"), P("dp", "tensor")),
        out_specs=P("dp", "tensor"),
        check_vma=False,
    )
```

```python
import jax
import jax.numpy as jnp
from jax import lax
from jax.sharding import PartitionSpec as P

epsilon = 1e-06
CHUNKS = 4


def gram_total(gram):
    n = gram.shape[0]
    flat = gram.reshape(-1, 128)
    flat = jnp.sum(lax.all_gather(flat, "dp"), axis=0)
    peers = jnp.broadcast_to(flat, (lax.axis_size("tensor"), *flat.shape))
    flat = jnp.sum(lax.all_to_all(peers, "tensor", 0, 0), axis=0)
    return flat.reshape(n, n)


def tree_weights(gram):
    n = gram.shape[0]
    index = jnp.arange(n)
    weights = jnp.ones((n,), jnp.float32)
    width = 1
    while width < n:
        scaled = gram * weights[:, None] * weights[None, :]
        item = index // width
        same = (item[:, None] == item[None, :])
        partner = (item[:, None] == (item ^ 1)[None, :])
        own = jnp.sum(jnp.where(same, scaled, 0.0), axis=1)
        cross = jnp.sum(jnp.where(partner, scaled, 0.0), axis=1)
        own = jnp.sum(jnp.where(same, own[None, :], 0.0), axis=1)
        cross = jnp.sum(jnp.where(same, cross[None, :], 0.0), axis=1)
        own = jnp.maximum(own, 0.0)
        weights = weights * (1.0 - cross / (2.0 * (own + epsilon)))
        width *= 2
    return weights


def on_device(activations, out_grads):
    replicas = lax.axis_size("dp")
    slabs = lax.axis_size("tensor")
    tokens, slab_rows = activations.shape
    columns = out_grads.shape[1]
    block_rows = slab_rows * slabs // replicas
    per_slab = slab_rows // block_rows
    rows = block_rows // CHUNKS
    x = activations.T.reshape(per_slab, CHUNKS, rows, tokens)
    blocks = []
    gram = jnp.zeros((replicas, replicas), jnp.float32)
    for chunk in range(CHUNKS):
        part = lax.all_gather(x[:, chunk], "tensor", axis=0)
        part = part.reshape(replicas * rows, tokens)
        grad = jnp.dot(part, out_grads, preferred_element_type=jnp.float32)
        grad = grad.reshape(replicas, rows, columns)
        block = lax.all_to_all(grad, "dp", 0, 0)
        blocks.append(block)
        gram = gram + lax.dot_general(
            block, block, (((1, 2), (1, 2)), ((), ())),
            precision=lax.Precision.HIGHEST, preferred_element_type=jnp.float32,
        )
    weights = tree_weights(gram_total(gram))
    out = [jnp.sum(b * weights[:, None, None], axis=0) for b in blocks]
    return jnp.concatenate(out, axis=0)


def solution(mesh):
    return jax.shard_map(
        on_device,
        mesh=mesh,
        in_specs=(P("dp", "tensor"), P("dp", "tensor")),
        out_specs=P("dp", "tensor"),
        check_vma=False,
    )
```

```python
import jax
import jax.numpy as jnp
from jax import lax
from jax.sharding import PartitionSpec as P

epsilon = 1e-06
GROUP_ENDS = (2, 4, 6, 8)


def gram_total(gram):
    n = gram.shape[0]
    flat = gram.reshape(-1, 128)
    flat = jnp.sum(lax.all_gather(flat, "dp"), axis=0)
    peers = jnp.broadcast_to(flat, (lax.axis_size("tensor"), *flat.shape))
    flat = jnp.sum(lax.all_to_all(peers, "tensor", 0, 0), axis=0)
    return flat.reshape(n, n)


def tree_weights(gram):
    n = gram.shape[0]
    index = jnp.arange(n)
    weights = jnp.ones((n,), jnp.float32)
    width = 1
    while width < n:
        scaled = gram * weights[:, None] * weights[None, :]
        item = index // width
        same = item[:, None] == item[None, :]
        partner = item[:, None] == (item ^ 1)[None, :]
        own = jnp.sum(jnp.where(same, scaled, 0.0), axis=1)
        cross = jnp.sum(jnp.where(partner, scaled, 0.0), axis=1)
        own = jnp.sum(jnp.where(same, own[None, :], 0.0), axis=1)
        cross = jnp.sum(jnp.where(same, cross[None, :], 0.0), axis=1)
        own = jnp.maximum(own, 0.0)
        weights = weights * (1.0 - cross / (2.0 * (own + epsilon)))
        width *= 2
    return weights


def on_device(activations, out_grads):
    replicas = lax.axis_size("dp")
    slabs = lax.axis_size("tensor")
    here = lax.axis_index("tensor")
    tokens, slab_rows = activations.shape
    columns = out_grads.shape[1]
    part = columns // replicas
    half = slabs // 2
    up = [(i, (i + 1) % slabs) for i in range(slabs)]
    down = [((i + 1) % slabs, i) for i in range(slabs)]

    slab = activations.T
    from_below = from_above = slab
    held, order = [slab], [0]
    blocks = []
    gram = jnp.zeros((replicas, replicas), jnp.float32)
    for step in range(1, half + 1):
        if step < half:
            from_below = lax.ppermute(from_below, "tensor", up)
            from_above = lax.ppermute(from_above, "tensor", down)
            held += [from_below, from_above]
            order += [slabs - step, step]
        else:
            cut = slab_rows // 2
            from_below = lax.ppermute(from_below[:cut], "tensor", up)
            from_above = lax.ppermute(from_above[cut:], "tensor", down)
            held += [from_below, from_above]
            order += [half]
        if step in GROUP_ENDS:
            group = jnp.concatenate(held, axis=0)
            grad = lax.dot_general(
                out_grads, group, (((0,), (1,)), ((), ())),
                preferred_element_type=jnp.float32,
            )
            block = lax.all_to_all(grad.reshape(replicas, part, -1), "dp", 0, 0)
            gram = gram + lax.dot_general(
                block, block, (((1, 2), (1, 2)), ((), ())),
                precision=lax.Precision.HIGHEST, preferred_element_type=jnp.float32,
            )
            blocks.append(block)
            held = []
    weights = tree_weights(gram_total(gram))
    sums = [jnp.sum(b * weights[:, None, None], axis=0) for b in blocks]
    by_slab = jnp.concatenate(sums, axis=1).reshape(part, slabs, slab_rows)
    by_slab = jnp.stack([by_slab[:, order.index(k)] for k in range(slabs)])
    by_slab = jnp.roll(by_slab, here, axis=0)
    home = by_slab.reshape(slabs, part, replicas // slabs, -1)
    home = home.transpose(0, 2, 1, 3).reshape(replicas, part, -1)
    home = lax.all_to_all(home, "dp", 0, 0)
    return home.reshape(columns, -1).T


def solution(mesh):
    return jax.shard_map(
        on_device,
        mesh=mesh,
        in_specs=(P("dp", "tensor"), P("dp", "tensor")),
        out_specs=P("dp", "tensor"),
        check_vma=False,
    )
```

```python
import functools

import jax
import jax.numpy as jnp
from jax import lax
from jax.experimental import pallas as pl
from jax.experimental.pallas import tpu as pltpu
from jax.sharding import PartitionSpec as P

epsilon = 1e-06
GROUPS = (6, 6, 4)
VMEM = pltpu.VMEM
LIMIT = 48 * 1024 * 1024
EXACT = lax.Precision.HIGHEST


def gram_kernel(replicas, block_ref, before_ref, out_ref):
    rows, cols = block_ref.shape
    part = rows // replicas
    whole = lax.dot_general(
        block_ref[...], block_ref[...], (((1,), (1,)), ((), ())),
        precision=EXACT, preferred_element_type=jnp.float32,
    )
    i = lax.broadcasted_iota(jnp.int32, (rows, rows), 0)
    j = lax.broadcasted_iota(jnp.int32, (rows, rows), 1)
    whole = jnp.where(i % part == j % part, whole, 0.0)
    thin = jnp.sum(whole.reshape(replicas, part, rows), axis=1)
    c = lax.broadcasted_iota(jnp.int32, (rows, 128), 0)
    lane = lax.broadcasted_iota(jnp.int32, (rows, 128), 1)
    total = before_ref[...]
    for k in range(replicas // 8):
        pick = jnp.where(lane == c // part + k * replicas, 1.0, 0.0)
        total = total + jnp.dot(
            thin[k * 8:(k + 1) * 8], pick,
            precision=EXACT, preferred_element_type=jnp.float32,
        )
    out_ref[...] = total


def gram_add(replicas, block, before):
    rows = block.shape[0] * block.shape[1]
    block = block.reshape(rows, -1)
    cols = block.shape[1]
    return pl.pallas_call(
        functools.partial(gram_kernel, replicas),
        out_shape=jax.ShapeDtypeStruct((8, 128), jnp.float32),
        in_specs=[pl.BlockSpec(memory_space=VMEM)] * 2,
        out_specs=pl.BlockSpec(memory_space=VMEM),
        cost_estimate=pl.CostEstimate(
            flops=12 * rows * rows * cols, bytes_accessed=4 * rows * cols, transcendentals=0
        ),
        compiler_params=pltpu.CompilerParams(vmem_limit_bytes=LIMIT),
    )(block, before)


def spread_kernel(parts_ref, out_ref):
    total = jnp.sum(parts_ref[...], axis=0)
    out_ref[...] = jnp.broadcast_to(total[None], out_ref.shape)


def sum_and_spread(parts, copies):
    return pl.pallas_call(
        spread_kernel,
        out_shape=jax.ShapeDtypeStruct((copies, *parts.shape[1:]), jnp.float32),
        in_specs=[pl.BlockSpec(memory_space=VMEM)],
        out_specs=pl.BlockSpec(memory_space=VMEM),
    )(parts)


def combine_kernel(replicas, slabs, order, here_ref, parts_ref, *refs):
    blocks, out_ref = refs[:-1], refs[-1]
    packed = jnp.sum(parts_ref[...], axis=0)
    gram = jnp.concatenate(
        [packed[:, k * replicas:(k + 1) * replicas] for k in range(replicas // 8)], axis=0
    )
    i = lax.broadcasted_iota(jnp.int32, (replicas, replicas), 0)
    j = lax.broadcasted_iota(jnp.int32, (replicas, replicas), 1)
    down = jnp.ones((replicas, 1), jnp.float32)
    across = jnp.ones((1, replicas), jnp.float32)
    width = 1
    while width < replicas:
        scaled = gram * down * across
        same = i // width == j // width
        partner = i // width == (j // width ^ 1)
        mine = jnp.where(same, scaled, 0.0)
        other = jnp.where(partner, scaled, 0.0)
        own_down = jnp.sum(mine, axis=1, keepdims=True)
        own_across = jnp.sum(mine, axis=0, keepdims=True)
        cross_down = jnp.sum(other, axis=1, keepdims=True)
        cross_across = jnp.sum(other, axis=0, keepdims=True)

        def factor(cross, own, axis):
            cross = jnp.sum(jnp.where(same, cross, 0.0), axis=axis, keepdims=True)
            own = jnp.sum(jnp.where(same, own, 0.0), axis=axis, keepdims=True)
            return 1.0 - cross / (2.0 * (jnp.maximum(own, 0.0) + epsilon))

        new_down = down * factor(cross_across, own_across, 1)
        across = across * factor(cross_down, own_down, 0)
        down = new_down
        width *= 2
    sums = []
    for block_ref in blocks:
        total = block_ref[0] * down[0:1]
        for r in range(1, replicas):
            total = total + block_ref[r] * down[r:r + 1]
        sums.append(total)
    each = replicas // slabs
    width = out_ref.shape[2]
    place = 0
    for total in sums:
        for k in range(total.shape[1] // (width * each)):
            slab = lax.rem(here_ref[0] + order[place], slabs)
            for h in range(each):
                start = (k * each + h) * width
                out_ref[slab * each + h] = total[:, start:start + width]
            place += 1


def weighted_sums(replicas, slabs, order, here, parts, blocks):
    part = blocks[0].shape[1]
    total = sum(b.shape[2] for b in blocks)
    size = replicas * part * total
    return pl.pallas_call(
        functools.partial(combine_kernel, replicas, slabs, order),
        out_shape=jax.ShapeDtypeStruct((replicas, part, total // replicas), jnp.float32),
        in_specs=[pl.BlockSpec(memory_space=pltpu.SMEM)]
        + [pl.BlockSpec(memory_space=VMEM)] * (1 + len(blocks)),
        out_specs=pl.BlockSpec(memory_space=VMEM),
        cost_estimate=pl.CostEstimate(flops=2 * size, bytes_accessed=4 * size, transcendentals=0),
        compiler_params=pltpu.CompilerParams(vmem_limit_bytes=LIMIT),
    )(here.reshape(1), parts, *blocks)


def on_device(activations, out_grads):
    replicas = lax.axis_size("dp")
    slabs = lax.axis_size("tensor")
    here = lax.axis_index("tensor").astype(jnp.int32)
    even = lax.axis_index("dp") % 2 == 0
    columns = out_grads.shape[1]
    part = columns // replicas
    half = slabs // 2
    up = [(i, (i + 1) % slabs) for i in range(slabs)]
    down = [((i + 1) % slabs, i) for i in range(slabs)]
    split = [
        (r * slabs + i, r * slabs + (i + (-1 if r % 2 else 1)) % slabs)
        for r in range(replicas) for i in range(slabs)
    ]

    slab = activations.T
    from_below = from_above = slab
    held, order = [slab], [0]
    blocks = []
    gram = jnp.zeros((8, 128), jnp.float32)
    sizes = list(GROUPS)
    for step in range(1, half + 1):
        if step < half:
            from_below = lax.ppermute(from_below, "tensor", up)
            from_above = lax.ppermute(from_above, "tensor", down)
            held += [from_below, from_above]
            order += [slabs - step, step]
        else:
            onward = jnp.where(even, from_below, from_above)
            held += [lax.ppermute(onward, ("dp", "tensor"), split)]
            order += [half]
        if len(held) >= sizes[0]:
            group, held = held[:sizes[0]], held[sizes.pop(0):]
            grad = lax.dot_general(
                out_grads, jnp.concatenate(group, axis=0), (((0,), (1,)), ((), ())),
                preferred_element_type=jnp.float32,
            )
            block = lax.all_to_all(grad.reshape(replicas, part, -1), "dp", 0, 0)
            gram = gram_add(replicas, block, gram)
            blocks.append(block)
    peers = jnp.broadcast_to(gram, (replicas, *gram.shape))
    parts = sum_and_spread(lax.all_to_all(peers, "dp", 0, 0), slabs)
    parts = lax.all_to_all(parts, "tensor", 0, 0)
    home = weighted_sums(replicas, slabs, tuple(order), here, parts, blocks)
    home = lax.all_to_all(home, "dp", 0, 0)
    return home.reshape(columns, -1).T


def solution(mesh):
    return jax.shard_map(
        on_device,
        mesh=mesh,
        in_specs=(P("dp", "tensor"), P("dp", "tensor")),
        out_specs=P("dp", "tensor"),
        check_vma=False,
    )
```

```python
import functools

import jax
import jax.numpy as jnp
from jax import lax
from jax.experimental import pallas as pl
from jax.experimental.pallas import tpu as pltpu
from jax.sharding import PartitionSpec as P

epsilon = 1e-06
PIECES = 2
GROUPS = (8, 8, 8, 8)
VMEM = pltpu.VMEM
LIMIT = 48 * 1024 * 1024
EXACT = lax.Precision.HIGHEST


def gram_kernel(replicas, block_ref, before_ref, out_ref):
    rows, cols = block_ref.shape
    part = rows // replicas
    whole = lax.dot_general(
        block_ref[...], block_ref[...], (((1,), (1,)), ((), ())),
        precision=EXACT, preferred_element_type=jnp.float32,
    )
    i = lax.broadcasted_iota(jnp.int32, (rows, rows), 0)
    j = lax.broadcasted_iota(jnp.int32, (rows, rows), 1)
    whole = jnp.where(i % part == j % part, whole, 0.0)
    thin = jnp.sum(whole.reshape(replicas, part, rows), axis=1)
    c = lax.broadcasted_iota(jnp.int32, (rows, 128), 0)
    lane = lax.broadcasted_iota(jnp.int32, (rows, 128), 1)
    total = before_ref[...]
    for k in range(replicas // 8):
        pick = jnp.where(lane == c // part + k * replicas, 1.0, 0.0)
        total = total + jnp.dot(
            thin[k * 8:(k + 1) * 8], pick,
            precision=EXACT, preferred_element_type=jnp.float32,
        )
    out_ref[...] = total


def gram_add(replicas, block, before):
    rows = block.shape[0] * block.shape[1]
    block = block.reshape(rows, -1)
    cols = block.shape[1]
    return pl.pallas_call(
        functools.partial(gram_kernel, replicas),
        out_shape=jax.ShapeDtypeStruct((8, 128), jnp.float32),
        in_specs=[pl.BlockSpec(memory_space=VMEM)] * 2,
        out_specs=pl.BlockSpec(memory_space=VMEM),
        cost_estimate=pl.CostEstimate(
            flops=12 * rows * rows * cols, bytes_accessed=4 * rows * cols, transcendentals=0
        ),
        compiler_params=pltpu.CompilerParams(vmem_limit_bytes=LIMIT),
    )(block, before)


def spread_kernel(parts_ref, out_ref):
    total = jnp.sum(parts_ref[...], axis=0)
    out_ref[...] = jnp.broadcast_to(total[None], out_ref.shape)


def sum_and_spread(parts, copies):
    return pl.pallas_call(
        spread_kernel,
        out_shape=jax.ShapeDtypeStruct((copies, *parts.shape[1:]), jnp.float32),
        in_specs=[pl.BlockSpec(memory_space=VMEM)],
        out_specs=pl.BlockSpec(memory_space=VMEM),
    )(parts)


def combine_kernel(replicas, slabs, order, here_ref, parts_ref, *refs):
    blocks, out_ref = refs[:-1], refs[-1]
    packed = jnp.sum(parts_ref[...], axis=0)
    gram = jnp.concatenate(
        [packed[:, k * replicas:(k + 1) * replicas] for k in range(replicas // 8)], axis=0
    )
    i = lax.broadcasted_iota(jnp.int32, (replicas, replicas), 0)
    j = lax.broadcasted_iota(jnp.int32, (replicas, replicas), 1)
    down = jnp.ones((replicas, 1), jnp.float32)
    across = jnp.ones((1, replicas), jnp.float32)
    width = 1
    while width < replicas:
        scaled = gram * down * across
        same = i // width == j // width
        partner = i // width == (j // width ^ 1)
        mine = jnp.where(same, scaled, 0.0)
        other = jnp.where(partner, scaled, 0.0)
        own_down = jnp.sum(mine, axis=1, keepdims=True)
        own_across = jnp.sum(mine, axis=0, keepdims=True)
        cross_down = jnp.sum(other, axis=1, keepdims=True)
        cross_across = jnp.sum(other, axis=0, keepdims=True)

        def factor(cross, own, axis):
            cross = jnp.sum(jnp.where(same, cross, 0.0), axis=axis, keepdims=True)
            own = jnp.sum(jnp.where(same, own, 0.0), axis=axis, keepdims=True)
            return 1.0 - cross / (2.0 * (jnp.maximum(own, 0.0) + epsilon))

        new_down = down * factor(cross_across, own_across, 1)
        across = across * factor(cross_down, own_down, 0)
        down = new_down
        width *= 2
    width = out_ref.shape[2]
    place = 0
    for block_ref in blocks:
        total = block_ref[0] * down[0:1]
        for r in range(1, replicas):
            total = total + block_ref[r] * down[r:r + 1]
        for start in range(0, total.shape[1], width):
            away, piece = order[place]
            slab = lax.rem(here_ref[0] + away, slabs)
            out_ref[slab * PIECES + piece] = total[:, start:start + width]
            place += 1


def weighted_sums(replicas, slabs, order, here, parts, blocks):
    part = blocks[0].shape[1]
    total = sum(b.shape[2] for b in blocks)
    size = replicas * part * total
    return pl.pallas_call(
        functools.partial(combine_kernel, replicas, slabs, order),
        out_shape=jax.ShapeDtypeStruct((replicas, part, total // replicas), jnp.float32),
        in_specs=[pl.BlockSpec(memory_space=pltpu.SMEM)]
        + [pl.BlockSpec(memory_space=VMEM)] * (1 + len(blocks)),
        out_specs=pl.BlockSpec(memory_space=VMEM),
        cost_estimate=pl.CostEstimate(flops=2 * size, bytes_accessed=4 * size, transcendentals=0),
        compiler_params=pltpu.CompilerParams(vmem_limit_bytes=LIMIT),
    )(here.reshape(1), parts, *blocks)


def on_device(activations, out_grads):
    replicas = lax.axis_size("dp")
    slabs = lax.axis_size("tensor")
    here = lax.axis_index("tensor").astype(jnp.int32)
    columns = out_grads.shape[1]
    part = columns // replicas
    half = slabs // 2
    up = [(i, (i + 1) % slabs) for i in range(slabs)]
    down = [((i + 1) % slabs, i) for i in range(slabs)]
    slab = activations.T
    rows = slab.shape[0] // PIECES
    pieces = [slab[i * rows:(i + 1) * rows] for i in range(PIECES)]
    below, above = list(pieces), list(pieces)
    held, order = list(pieces), [(0, i) for i in range(PIECES)]
    blocks = []
    gram = jnp.zeros((8, 128), jnp.float32)
    sizes = list(GROUPS)
    for step in range(1, half + 1):
        for i in range(PIECES):
            if step < half or i < PIECES // 2:
                below[i] = lax.ppermute(below[i], "tensor", up)
                held.append(below[i])
                order.append((slabs - step, i))
            if step < half or i >= PIECES // 2:
                above[i] = lax.ppermute(above[i], "tensor", down)
                held.append(above[i])
                order.append((step, i))
        if len(held) >= sizes[0]:
            group, held = held[:sizes[0]], held[sizes.pop(0):]
            grad = lax.dot_general(
                out_grads, jnp.concatenate(group, axis=0), (((0,), (1,)), ((), ())),
                preferred_element_type=jnp.float32,
            )
            block = lax.all_to_all(grad.reshape(replicas, part, -1), "dp", 0, 0)
            gram = gram_add(replicas, block, gram)
            blocks.append(block)
    peers = jnp.broadcast_to(gram, (replicas, *gram.shape))
    parts = sum_and_spread(lax.all_to_all(peers, "dp", 0, 0), slabs)
    parts = lax.all_to_all(parts, "tensor", 0, 0)
    home = weighted_sums(replicas, slabs, tuple(order), here, parts, blocks)
    home = lax.all_to_all(home, "dp", 0, 0)
    return home.reshape(columns, -1).T


def solution(mesh):
    return jax.shard_map(
        on_device,
        mesh=mesh,
        in_specs=(P("dp", "tensor"), P("dp", "tensor")),
        out_specs=P("dp", "tensor"),
        check_vma=False,
    )
```

```python
import functools

import jax
import jax.numpy as jnp
from jax import lax
from jax.experimental import pallas as pl
from jax.experimental.pallas import tpu as pltpu
from jax.sharding import PartitionSpec as P

epsilon = 1e-06
GROUPS = (4, 4, 4, 4)
VMEM = pltpu.VMEM
LIMIT = 48 * 1024 * 1024
EXACT = lax.Precision.HIGHEST


def gram_kernel(replicas, block_ref, before_ref, out_ref):
    part = block_ref.shape[1] // 4
    rows = replicas * part
    i = lax.broadcasted_iota(jnp.int32, (rows, rows), 0)
    j = lax.broadcasted_iota(jnp.int32, (rows, rows), 1)
    whole = jnp.zeros((rows, rows), jnp.float32)
    for core in range(2):
        first = block_ref[:, (3 * core) * part:(3 * core + 1) * part]
        second = block_ref[:, (1 + core) * part:(2 + core) * part]
        both = jnp.concatenate([first, second], axis=1).reshape(rows, -1)
        whole = whole + lax.dot_general(
            both, both, (((1,), (1,)), ((), ())),
            precision=EXACT, preferred_element_type=jnp.float32,
        )
    whole = jnp.where(i % part == j % part, whole, 0.0)
    thin = jnp.sum(whole.reshape(replicas, part, rows), axis=1)
    c = lax.broadcasted_iota(jnp.int32, (rows, 128), 0)
    lane = lax.broadcasted_iota(jnp.int32, (rows, 128), 1)
    total = before_ref[...]
    for k in range(replicas // 8):
        pick = jnp.where(lane == c // part + k * replicas, 1.0, 0.0)
        total = total + jnp.dot(
            thin[k * 8:(k + 1) * 8], pick,
            precision=EXACT, preferred_element_type=jnp.float32,
        )
    out_ref[...] = total


def gram_add(replicas, block, before):
    block = block.reshape(replicas // 2, 2 * block.shape[1], -1)
    size = block.size
    return pl.pallas_call(
        functools.partial(gram_kernel, replicas),
        out_shape=jax.ShapeDtypeStruct((8, 128), jnp.float32),
        in_specs=[pl.BlockSpec(memory_space=VMEM)] * 2,
        out_specs=pl.BlockSpec(memory_space=VMEM),
        cost_estimate=pl.CostEstimate(
            flops=12 * size * replicas * 8, bytes_accessed=4 * size, transcendentals=0
        ),
        compiler_params=pltpu.CompilerParams(vmem_limit_bytes=LIMIT),
    )(block, before)


def spread_kernel(parts_ref, out_ref):
    total = jnp.sum(parts_ref[...], axis=0)
    out_ref[...] = jnp.broadcast_to(total[None], out_ref.shape)


def sum_and_spread(parts, copies):
    return pl.pallas_call(
        spread_kernel,
        out_shape=jax.ShapeDtypeStruct((copies, *parts.shape[1:]), jnp.float32),
        in_specs=[pl.BlockSpec(memory_space=VMEM)],
        out_specs=pl.BlockSpec(memory_space=VMEM),
    )(parts)


def combine_kernel(replicas, slabs, order, here_ref, parts_ref, *refs):
    blocks, out_ref = refs[:-1], refs[-1]
    packed = jnp.sum(parts_ref[...], axis=0)
    gram = jnp.concatenate(
        [packed[:, k * replicas:(k + 1) * replicas] for k in range(replicas // 8)], axis=0
    )
    i = lax.broadcasted_iota(jnp.int32, (replicas, replicas), 0)
    j = lax.broadcasted_iota(jnp.int32, (replicas, replicas), 1)
    down = jnp.ones((replicas, 1), jnp.float32)
    across = jnp.ones((1, replicas), jnp.float32)
    width = 1
    while width < replicas:
        scaled = gram * down * across
        same = i // width == j // width
        partner = i // width == (j // width ^ 1)
        mine = jnp.where(same, scaled, 0.0)
        other = jnp.where(partner, scaled, 0.0)
        own_down = jnp.sum(mine, axis=1, keepdims=True)
        own_across = jnp.sum(mine, axis=0, keepdims=True)
        cross_down = jnp.sum(other, axis=1, keepdims=True)
        cross_across = jnp.sum(other, axis=0, keepdims=True)

        def factor(cross, own, axis):
            cross = jnp.sum(jnp.where(same, cross, 0.0), axis=axis, keepdims=True)
            own = jnp.sum(jnp.where(same, own, 0.0), axis=axis, keepdims=True)
            return 1.0 - cross / (2.0 * (jnp.maximum(own, 0.0) + epsilon))

        new_down = down * factor(cross_across, own_across, 1)
        across = across * factor(cross_down, own_down, 0)
        down = new_down
        width *= 2
    part, width = out_ref.shape[1:]
    for core in range(2):
        place = 0
        for block_ref in blocks:
            total = 0.0
            for r in range(replicas):
                row = (r + core) % 2 * part
                total = total + block_ref[r // 2 * 2 + core, row:row + part] * down[r:r + 1]
            for start in range(0, total.shape[1], width):
                away, piece = order[core][place]
                slab = lax.rem(here_ref[0] + away, slabs)
                out_ref[slab * 2 + piece] = total[:, start:start + width]
                place += 1


def weighted_sums(replicas, slabs, order, here, parts, blocks):
    part = blocks[0].shape[1] // 2
    total = 2 * sum(b.shape[2] for b in blocks)
    size = replicas * part * total
    return pl.pallas_call(
        functools.partial(combine_kernel, replicas, slabs, order),
        out_shape=jax.ShapeDtypeStruct((replicas, part, total // replicas), jnp.float32),
        in_specs=[pl.BlockSpec(memory_space=pltpu.SMEM)]
        + [pl.BlockSpec(memory_space=VMEM)] * (1 + len(blocks)),
        out_specs=pl.BlockSpec(memory_space=VMEM),
        cost_estimate=pl.CostEstimate(flops=2 * size, bytes_accessed=4 * size, transcendentals=0),
        compiler_params=pltpu.CompilerParams(vmem_limit_bytes=LIMIT),
    )(here.reshape(1), parts, *blocks)


def on_device(activations, out_grads):
    replicas = lax.axis_size("dp")
    slabs = lax.axis_size("tensor")
    here = lax.axis_index("tensor").astype(jnp.int32)
    core = lax.axis_index("dp") % 2
    tokens, slab_rows = activations.shape
    columns = out_grads.shape[1]
    part = columns // replicas
    half = slabs // 2
    rows = slab_rows // 2
    sibling = [(r, r ^ 1) for r in range(replicas)]
    onward = [
        (r * slabs + i, r * slabs + (i + (-1 if r % 2 else 1)) % slabs)
        for r in range(replicas) for i in range(slabs)
    ]

    def own_half(slab):
        return lax.dynamic_slice(slab, (core * rows, 0), (rows, tokens))

    def move(slab):
        return lax.ppermute(slab, ("dp", "tensor"), onward)

    mine = activations.T
    chains = [mine, lax.ppermute(mine, "dp", sibling)]
    grads = [out_grads, lax.ppermute(out_grads, "dp", sibling)]
    held = [[own_half(slab)] for slab in chains]
    order = [[(0, 0)], [(0, 1)]]
    blocks = []
    gram = jnp.zeros((8, 128), jnp.float32)
    sizes = list(GROUPS)
    for step in range(1, half + 1):
        if step < half:
            chains = [move(slab) for slab in chains]
            for k in range(2):
                held[k] += [chains[k][:rows], chains[k][rows:]]
            order[0] += [(slabs - step, 0), (slabs - step, 1)]
            order[1] += [(step, 0), (step, 1)]
        else:
            for k in range(2):
                held[k].append(move(own_half(chains[k])))
                order[k].append((half, k))
        if len(held[0]) >= sizes[0]:
            count = sizes.pop(0)
            parts = []
            for k in range(2):
                group, held[k] = held[k][:count], held[k][count:]
                grad = lax.dot_general(
                    grads[k], jnp.concatenate(group, axis=0), (((0,), (1,)), ((), ())),
                    preferred_element_type=jnp.float32,
                )
                parts.append(grad.reshape(replicas, part, -1))
            block = lax.all_to_all(jnp.concatenate(parts, axis=1), "dp", 0, 0)
            gram = gram_add(replicas, block, gram)
            blocks.append(block)
    peers = jnp.broadcast_to(gram, (replicas, *gram.shape))
    parts = sum_and_spread(lax.all_to_all(peers, "dp", 0, 0), slabs)
    parts = lax.all_to_all(parts, "tensor", 0, 0)
    home = weighted_sums(replicas, slabs, order, here, parts, blocks)
    home = lax.all_to_all(home, "dp", 0, 0)
    return home.reshape(columns, -1).T


def solution(mesh):
    return jax.shard_map(
        on_device,
        mesh=mesh,
        in_specs=(P("dp", "tensor"), P("dp", "tensor")),
        out_specs=P("dp", "tensor"),
        check_vma=False,
    )
```

```python
import functools

import jax
import jax.numpy as jnp
from jax import lax
from jax.experimental import pallas as pl
from jax.experimental.pallas import tpu as pltpu
from jax.sharding import PartitionSpec as P

epsilon = 1e-06
GROUPS = (4, 4, 4, 4)
VMEM = pltpu.VMEM
LIMIT = 48 * 1024 * 1024
EXACT = lax.Precision.HIGHEST


def gram_kernel(replicas, block_ref, before_ref, out_ref):
    part = block_ref.shape[1] // 4
    rows = replicas * part
    i = lax.broadcasted_iota(jnp.int32, (rows, rows), 0)
    j = lax.broadcasted_iota(jnp.int32, (rows, rows), 1)
    whole = jnp.zeros((rows, rows), jnp.float32)
    for core in range(2):
        first = block_ref[:, (3 * core) * part:(3 * core + 1) * part]
        second = block_ref[:, (1 + core) * part:(2 + core) * part]
        both = jnp.concatenate([first, second], axis=1).reshape(rows, -1)
        whole = whole + lax.dot_general(
            both, both, (((1,), (1,)), ((), ())),
            precision=EXACT, preferred_element_type=jnp.float32,
        )
    whole = jnp.where(i % part == j % part, whole, 0.0)
    thin = jnp.sum(whole.reshape(replicas, part, rows), axis=1)
    c = lax.broadcasted_iota(jnp.int32, (rows, 128), 0)
    lane = lax.broadcasted_iota(jnp.int32, (rows, 128), 1)
    total = before_ref[...]
    for k in range(replicas // 8):
        pick = jnp.where(lane == c // part + k * replicas, 1.0, 0.0)
        total = total + jnp.dot(
            thin[k * 8:(k + 1) * 8], pick,
            precision=EXACT, preferred_element_type=jnp.float32,
        )
    out_ref[...] = total


def gram_add(replicas, block, before):
    block = block.reshape(replicas // 2, 2 * block.shape[1], -1)
    size = block.size
    return pl.pallas_call(
        functools.partial(gram_kernel, replicas),
        out_shape=jax.ShapeDtypeStruct((8, 128), jnp.float32),
        in_specs=[pl.BlockSpec(memory_space=VMEM)] * 2,
        out_specs=pl.BlockSpec(memory_space=VMEM),
        cost_estimate=pl.CostEstimate(
            flops=12 * size * replicas * 8, bytes_accessed=4 * size, transcendentals=0
        ),
        compiler_params=pltpu.CompilerParams(vmem_limit_bytes=LIMIT),
    )(block, before)


def spread_kernel(parts_ref, out_ref):
    total = jnp.sum(parts_ref[...], axis=0)
    out_ref[...] = jnp.broadcast_to(total[None], out_ref.shape)


def sum_and_spread(parts, copies):
    return pl.pallas_call(
        spread_kernel,
        out_shape=jax.ShapeDtypeStruct((copies, *parts.shape[1:]), jnp.float32),
        in_specs=[pl.BlockSpec(memory_space=VMEM)],
        out_specs=pl.BlockSpec(memory_space=VMEM),
    )(parts)


def combine_kernel(replicas, slabs, order, here_ref, parts_ref, *refs):
    blocks, out_ref = refs[:-1], refs[-1]
    packed = jnp.sum(parts_ref[...], axis=0)
    gram = jnp.concatenate(
        [packed[:, k * replicas:(k + 1) * replicas] for k in range(replicas // 8)], axis=0
    )
    i = lax.broadcasted_iota(jnp.int32, (replicas, replicas), 0)
    j = lax.broadcasted_iota(jnp.int32, (replicas, replicas), 1)
    down = jnp.ones((replicas, 1), jnp.float32)
    across = jnp.ones((1, replicas), jnp.float32)
    width = 1
    while width < replicas:
        scaled = gram * down * across
        same = i // width == j // width
        partner = i // width == (j // width ^ 1)
        mine = jnp.where(same, scaled, 0.0)
        other = jnp.where(partner, scaled, 0.0)
        own_down = jnp.sum(mine, axis=1, keepdims=True)
        own_across = jnp.sum(mine, axis=0, keepdims=True)
        cross_down = jnp.sum(other, axis=1, keepdims=True)
        cross_across = jnp.sum(other, axis=0, keepdims=True)

        def factor(cross, own, axis):
            cross = jnp.sum(jnp.where(same, cross, 0.0), axis=axis, keepdims=True)
            own = jnp.sum(jnp.where(same, own, 0.0), axis=axis, keepdims=True)
            return 1.0 - cross / (2.0 * (jnp.maximum(own, 0.0) + epsilon))

        new_down = down * factor(cross_across, own_across, 1)
        across = across * factor(cross_down, own_down, 0)
        down = new_down
        width *= 2
    part, width = out_ref.shape[1:]
    for core in range(2):
        place = 0
        for block_ref in blocks:
            total = 0.0
            for r in range(replicas):
                row = (r + core) % 2 * part
                total = total + block_ref[r // 2 * 2 + core, row:row + part] * down[r:r + 1]
            for start in range(0, total.shape[1], width):
                away, piece = order[core][place]
                slab = lax.rem(here_ref[0] + away, slabs)
                out_ref[slab * 2 + piece] = total[:, start:start + width]
                place += 1


def weighted_sums(replicas, slabs, order, here, parts, blocks):
    part = blocks[0].shape[1] // 2
    total = 2 * sum(b.shape[2] for b in blocks)
    size = replicas * part * total
    return pl.pallas_call(
        functools.partial(combine_kernel, replicas, slabs, order),
        out_shape=jax.ShapeDtypeStruct((replicas, part, total // replicas), jnp.float32),
        in_specs=[pl.BlockSpec(memory_space=pltpu.SMEM)]
        + [pl.BlockSpec(memory_space=VMEM)] * (1 + len(blocks)),
        out_specs=pl.BlockSpec(memory_space=VMEM),
        cost_estimate=pl.CostEstimate(flops=2 * size, bytes_accessed=4 * size, transcendentals=0),
        compiler_params=pltpu.CompilerParams(vmem_limit_bytes=LIMIT),
    )(here.reshape(1), parts, *blocks)


def on_device(activations, out_grads):
    replicas = lax.axis_size("dp")
    slabs = lax.axis_size("tensor")
    here = lax.axis_index("tensor").astype(jnp.int32)
    core = lax.axis_index("dp") % 2
    tokens, slab_rows = activations.shape
    columns = out_grads.shape[1]
    part = columns // replicas
    half = slabs // 2
    rows = slab_rows // 2
    sibling = [(r, r ^ 1) for r in range(replicas)]
    onward = [
        (r * slabs + i, r * slabs + (i + (-1 if r % 2 else 1)) % slabs)
        for r in range(replicas) for i in range(slabs)
    ]

    def own_half(slab):
        return lax.dynamic_slice(slab, (core * rows, 0), (rows, tokens))

    def move(slab):
        return lax.ppermute(slab, ("dp", "tensor"), onward)

    mine = activations.T
    chains = [mine, lax.ppermute(mine, "dp", sibling)]
    grads = [out_grads, lax.ppermute(out_grads, "dp", sibling)]
    chains[1], grads[1] = lax.optimization_barrier((chains[1], grads[1]))
    held = [[own_half(slab)] for slab in chains]
    order = [[(0, 0)], [(0, 1)]]
    blocks = []
    gram = jnp.zeros((8, 128), jnp.float32)
    sizes = list(GROUPS)
    ready = None
    for step in range(1, half + 1):
        if step < half:
            chains = [move(slab) for slab in chains]
            if ready is not None:
                chains[0], ready = lax.optimization_barrier((chains[0], ready))
                blocks.append(lax.all_to_all(ready, "dp", 0, 0))
                ready = None
            for k in range(2):
                held[k] += [chains[k][:rows], chains[k][rows:]]
            order[0] += [(slabs - step, 0), (slabs - step, 1)]
            order[1] += [(step, 0), (step, 1)]
        else:
            for k in range(2):
                held[k].append(move(own_half(chains[k])))
                order[k].append((half, k))
        if len(held[0]) >= sizes[0]:
            count = sizes.pop(0)
            parts = []
            for k in range(2):
                group, held[k] = held[k][:count], held[k][count:]
                grad = lax.dot_general(
                    grads[k], jnp.concatenate(group, axis=0), (((0,), (1,)), ((), ())),
                    preferred_element_type=jnp.float32,
                )
                parts.append(grad.reshape(replicas, part, -1))
            ready = jnp.concatenate(parts, axis=1)
    blocks.append(lax.all_to_all(ready, "dp", 0, 0))
    for block in blocks:
        gram = gram_add(replicas, block, gram)
    peers = jnp.broadcast_to(gram, (replicas, *gram.shape))
    parts = sum_and_spread(lax.all_to_all(peers, "dp", 0, 0), slabs)
    parts = lax.all_to_all(parts, "tensor", 0, 0)
    home = weighted_sums(replicas, slabs, order, here, parts, blocks)
    home = lax.all_to_all(home, "dp", 0, 0)
    return home.reshape(columns, -1).T


def solution(mesh):
    return jax.shard_map(
        on_device,
        mesh=mesh,
        in_specs=(P("dp", "tensor"), P("dp", "tensor")),
        out_specs=P("dp", "tensor"),
        check_vma=False,
    )
```

```python
import functools

import jax
import jax.numpy as jnp
from jax import lax
from jax.experimental import pallas as pl
from jax.experimental.pallas import tpu as pltpu
from jax.sharding import PartitionSpec as P

epsilon = 1e-06
GROUPS = (768, 896, 896)
TIES = {(5, 0): 0}
VMEM = pltpu.VMEM
LIMIT = 48 * 1024 * 1024
EXACT = lax.Precision.HIGHEST


def gram_kernel(replicas, block_ref, before_ref, out_ref):
    part = block_ref.shape[1] // 4
    rows = replicas * part
    i = lax.broadcasted_iota(jnp.int32, (rows, rows), 0)
    j = lax.broadcasted_iota(jnp.int32, (rows, rows), 1)
    whole = jnp.zeros((rows, rows), jnp.float32)
    for core in range(2):
        first = block_ref[:, (3 * core) * part:(3 * core + 1) * part]
        second = block_ref[:, (1 + core) * part:(2 + core) * part]
        both = jnp.concatenate([first, second], axis=1).reshape(rows, -1)
        whole = whole + lax.dot_general(
            both, both, (((1,), (1,)), ((), ())),
            precision=EXACT, preferred_element_type=jnp.float32,
        )
    whole = jnp.where(i % part == j % part, whole, 0.0)
    thin = jnp.sum(whole.reshape(replicas, part, rows), axis=1)
    c = lax.broadcasted_iota(jnp.int32, (rows, 128), 0)
    lane = lax.broadcasted_iota(jnp.int32, (rows, 128), 1)
    total = before_ref[...]
    for k in range(replicas // 8):
        pick = jnp.where(lane == c // part + k * replicas, 1.0, 0.0)
        total = total + jnp.dot(
            thin[k * 8:(k + 1) * 8], pick,
            precision=EXACT, preferred_element_type=jnp.float32,
        )
    out_ref[...] = total


def gram_add(replicas, block, before):
    block = block.reshape(replicas // 2, 2 * block.shape[1], -1)
    size = block.size
    return pl.pallas_call(
        functools.partial(gram_kernel, replicas),
        out_shape=jax.ShapeDtypeStruct((8, 128), jnp.float32),
        in_specs=[pl.BlockSpec(memory_space=VMEM)] * 2,
        out_specs=pl.BlockSpec(memory_space=VMEM),
        cost_estimate=pl.CostEstimate(
            flops=12 * size * replicas * 8, bytes_accessed=4 * size, transcendentals=0
        ),
        compiler_params=pltpu.CompilerParams(vmem_limit_bytes=LIMIT),
    )(block, before)


def spread_kernel(parts_ref, out_ref):
    total = jnp.sum(parts_ref[...], axis=0)
    out_ref[...] = jnp.broadcast_to(total[None], out_ref.shape)


def sum_and_spread(parts, copies):
    return pl.pallas_call(
        spread_kernel,
        out_shape=jax.ShapeDtypeStruct((copies, *parts.shape[1:]), jnp.float32),
        in_specs=[pl.BlockSpec(memory_space=VMEM)],
        out_specs=pl.BlockSpec(memory_space=VMEM),
    )(parts)


def combine_kernel(replicas, slabs, order, here_ref, parts_ref, *refs):
    blocks, out_ref = refs[:-1], refs[-1]
    packed = jnp.sum(parts_ref[...], axis=0)
    gram = jnp.concatenate(
        [packed[:, k * replicas:(k + 1) * replicas] for k in range(replicas // 8)], axis=0
    )
    i = lax.broadcasted_iota(jnp.int32, (replicas, replicas), 0)
    j = lax.broadcasted_iota(jnp.int32, (replicas, replicas), 1)
    down = jnp.ones((replicas, 1), jnp.float32)
    across = jnp.ones((1, replicas), jnp.float32)
    width = 1
    while width < replicas:
        scaled = gram * down * across
        same = i // width == j // width
        partner = i // width == (j // width ^ 1)
        mine = jnp.where(same, scaled, 0.0)
        other = jnp.where(partner, scaled, 0.0)
        own_down = jnp.sum(mine, axis=1, keepdims=True)
        own_across = jnp.sum(mine, axis=0, keepdims=True)
        cross_down = jnp.sum(other, axis=1, keepdims=True)
        cross_across = jnp.sum(other, axis=0, keepdims=True)

        def factor(cross, own, axis):
            cross = jnp.sum(jnp.where(same, cross, 0.0), axis=axis, keepdims=True)
            own = jnp.sum(jnp.where(same, own, 0.0), axis=axis, keepdims=True)
            return 1.0 - cross / (2.0 * (jnp.maximum(own, 0.0) + epsilon))

        new_down = down * factor(cross_across, own_across, 1)
        across = across * factor(cross_down, own_down, 0)
        down = new_down
        width *= 2
    part, width = out_ref.shape[1:]
    for core in range(2):
        sums = []
        for block_ref in blocks:
            total = 0.0
            for r in range(replicas):
                row = (r + core) % 2 * part
                total = total + block_ref[r // 2 * 2 + core, row:row + part] * down[r:r + 1]
            sums.append(total)
        sums = jnp.concatenate(sums, axis=1)
        for place, (away, piece) in enumerate(order[core]):
            slab = lax.rem(here_ref[0] + away, slabs)
            out_ref[slab * 2 + piece] = sums[:, place * width:(place + 1) * width]


def weighted_sums(replicas, slabs, order, here, parts, blocks):
    part = blocks[0].shape[1] // 2
    total = 2 * sum(b.shape[2] for b in blocks)
    size = replicas * part * total
    return pl.pallas_call(
        functools.partial(combine_kernel, replicas, slabs, order),
        out_shape=jax.ShapeDtypeStruct((replicas, part, total // replicas), jnp.float32),
        in_specs=[pl.BlockSpec(memory_space=pltpu.SMEM)]
        + [pl.BlockSpec(memory_space=VMEM)] * (1 + len(blocks)),
        out_specs=pl.BlockSpec(memory_space=VMEM),
        cost_estimate=pl.CostEstimate(flops=2 * size, bytes_accessed=4 * size, transcendentals=0),
        compiler_params=pltpu.CompilerParams(vmem_limit_bytes=LIMIT),
    )(here.reshape(1), parts, *blocks)


def on_device(activations, out_grads):
    replicas = lax.axis_size("dp")
    slabs = lax.axis_size("tensor")
    here = lax.axis_index("tensor").astype(jnp.int32)
    core = lax.axis_index("dp") % 2
    tokens, slab_rows = activations.shape
    columns = out_grads.shape[1]
    part = columns // replicas
    half = slabs // 2
    rows = slab_rows // 2
    sibling = [(r, r ^ 1) for r in range(replicas)]
    onward = [
        (r * slabs + i, r * slabs + (i + (-1 if r % 2 else 1)) % slabs)
        for r in range(replicas) for i in range(slabs)
    ]

    def own_half(slab):
        return lax.dynamic_slice(slab, (core * rows, 0), (rows, tokens))

    def move(slab):
        return lax.ppermute(slab, ("dp", "tensor"), onward)

    def take(pieces, count):
        taken = []
        while count:
            piece = pieces[0]
            size = min(count, piece.shape[0])
            taken.append(piece[:size])
            count -= size
            pieces = [piece[size:]][: piece.shape[0] > size] + pieces[1:]
        return jnp.concatenate(taken, axis=0), pieces

    mine = activations.T
    chains = [mine, lax.ppermute(mine, "dp", sibling)]
    grads = [out_grads, out_grads]
    chains[1], grads[1] = lax.optimization_barrier((chains[1], grads[1]))
    grads[1] = lax.ppermute(grads[1], "dp", sibling)
    held = [[own_half(slab)] for slab in chains]
    order = [[(0, 0)], [(0, 1)]]
    blocks = []
    gram = jnp.zeros((8, 128), jnp.float32)
    sizes = list(GROUPS)
    for step in range(1, half + 1):
        if step < half:
            chains = [move(slab) for slab in chains]
            if step == 1:
                chains[1], grads[1] = lax.optimization_barrier((chains[1], grads[1]))
            for k in range(2):
                if (step, k) in TIES:
                    place = TIES[step, k]
                    chains[k], blocks[place] = lax.optimization_barrier((chains[k], blocks[place]))
                held[k].append(chains[k])
            order[0] += [(slabs - step, 0), (slabs - step, 1)]
            order[1] += [(step, 0), (step, 1)]
        else:
            for k in range(2):
                held[k].append(move(own_half(chains[k])))
                order[k].append((half, k))
        if sum(piece.shape[0] for piece in held[0]) >= sizes[0]:
            count = sizes.pop(0)
            parts = []
            for k in range(2):
                group, held[k] = take(held[k], count)
                grad = lax.dot_general(
                    grads[k], group, (((0,), (1,)), ((), ())),
                    preferred_element_type=jnp.float32,
                )
                parts.append(grad.reshape(replicas, part, -1))
            ready = jnp.concatenate(parts, axis=1)
            if step < half:
                chains[1], ready = lax.optimization_barrier((chains[1], ready))
            blocks.append(lax.all_to_all(ready, "dp", 0, 0))
    for block in blocks:
        gram = gram_add(replicas, block, gram)
    peers = jnp.broadcast_to(gram, (replicas, *gram.shape))
    parts = sum_and_spread(lax.all_to_all(peers, "dp", 0, 0), slabs)
    parts = lax.all_to_all(parts, "tensor", 0, 0)
    home = weighted_sums(replicas, slabs, order, here, parts, blocks)
    home = lax.all_to_all(home, "dp", 0, 0)
    return home.reshape(columns, -1).T


def solution(mesh):
    return jax.shard_map(
        on_device,
        mesh=mesh,
        in_specs=(P("dp", "tensor"), P("dp", "tensor")),
        out_specs=P("dp", "tensor"),
        check_vma=False,
    )
```

```python
import functools

import jax
import jax.numpy as jnp
from jax import lax
from jax.experimental import pallas as pl
from jax.experimental.pallas import tpu as pltpu
from jax.sharding import PartitionSpec as P

epsilon = 1e-06
GROUPS = (768, 640, 640, 512)
TIES = {(4, 1): 0, (6, 1): 1}
VMEM = pltpu.VMEM
LIMIT = 48 * 1024 * 1024
EXACT = lax.Precision.HIGHEST


def gram_kernel(replicas, block_ref, before_ref, out_ref):
    part = block_ref.shape[1] // 4
    rows = replicas * part
    i = lax.broadcasted_iota(jnp.int32, (rows, rows), 0)
    j = lax.broadcasted_iota(jnp.int32, (rows, rows), 1)
    whole = jnp.zeros((rows, rows), jnp.float32)
    for core in range(2):
        first = block_ref[:, (3 * core) * part:(3 * core + 1) * part]
        second = block_ref[:, (1 + core) * part:(2 + core) * part]
        both = jnp.concatenate([first, second], axis=1).reshape(rows, -1)
        whole = whole + lax.dot_general(
            both, both, (((1,), (1,)), ((), ())),
            precision=EXACT, preferred_element_type=jnp.float32,
        )
    whole = jnp.where(i % part == j % part, whole, 0.0)
    thin = jnp.sum(whole.reshape(replicas, part, rows), axis=1)
    c = lax.broadcasted_iota(jnp.int32, (rows, 128), 0)
    lane = lax.broadcasted_iota(jnp.int32, (rows, 128), 1)
    total = before_ref[...]
    for k in range(replicas // 8):
        pick = jnp.where(lane == c // part + k * replicas, 1.0, 0.0)
        total = total + jnp.dot(
            thin[k * 8:(k + 1) * 8], pick,
            precision=EXACT, preferred_element_type=jnp.float32,
        )
    out_ref[...] = total


def gram_add(replicas, block, before):
    block = block.reshape(replicas // 2, 2 * block.shape[1], -1)
    size = block.size
    return pl.pallas_call(
        functools.partial(gram_kernel, replicas),
        out_shape=jax.ShapeDtypeStruct((8, 128), jnp.float32),
        in_specs=[pl.BlockSpec(memory_space=VMEM)] * 2,
        out_specs=pl.BlockSpec(memory_space=VMEM),
        cost_estimate=pl.CostEstimate(
            flops=12 * size * replicas * 8, bytes_accessed=4 * size, transcendentals=0
        ),
        compiler_params=pltpu.CompilerParams(vmem_limit_bytes=LIMIT),
    )(block, before)


def spread_kernel(parts_ref, out_ref):
    total = jnp.sum(parts_ref[...], axis=0)
    out_ref[...] = jnp.broadcast_to(total[None], out_ref.shape)


def sum_and_spread(parts, copies):
    return pl.pallas_call(
        spread_kernel,
        out_shape=jax.ShapeDtypeStruct((copies, *parts.shape[1:]), jnp.float32),
        in_specs=[pl.BlockSpec(memory_space=VMEM)],
        out_specs=pl.BlockSpec(memory_space=VMEM),
    )(parts)


def combine_kernel(replicas, slabs, order, here_ref, parts_ref, *refs):
    blocks, out_ref = refs[:-1], refs[-1]
    packed = jnp.sum(parts_ref[...], axis=0)
    gram = jnp.concatenate(
        [packed[:, k * replicas:(k + 1) * replicas] for k in range(replicas // 8)], axis=0
    )
    i = lax.broadcasted_iota(jnp.int32, (replicas, replicas), 0)
    j = lax.broadcasted_iota(jnp.int32, (replicas, replicas), 1)
    down = jnp.ones((replicas, 1), jnp.float32)
    across = jnp.ones((1, replicas), jnp.float32)
    width = 1
    while width < replicas:
        scaled = gram * down * across
        same = i // width == j // width
        partner = i // width == (j // width ^ 1)
        mine = jnp.where(same, scaled, 0.0)
        other = jnp.where(partner, scaled, 0.0)
        own_down = jnp.sum(mine, axis=1, keepdims=True)
        own_across = jnp.sum(mine, axis=0, keepdims=True)
        cross_down = jnp.sum(other, axis=1, keepdims=True)
        cross_across = jnp.sum(other, axis=0, keepdims=True)

        def factor(cross, own, axis):
            cross = jnp.sum(jnp.where(same, cross, 0.0), axis=axis, keepdims=True)
            own = jnp.sum(jnp.where(same, own, 0.0), axis=axis, keepdims=True)
            return 1.0 - cross / (2.0 * (jnp.maximum(own, 0.0) + epsilon))

        new_down = down * factor(cross_across, own_across, 1)
        across = across * factor(cross_down, own_down, 0)
        down = new_down
        width *= 2
    part, width = out_ref.shape[1:]
    for core in range(2):
        sums = []
        for block_ref in blocks:
            total = 0.0
            for r in range(replicas):
                row = (r + core) % 2 * part
                total = total + block_ref[r // 2 * 2 + core, row:row + part] * down[r:r + 1]
            sums.append(total)
        sums = jnp.concatenate(sums, axis=1)
        for place, (away, piece) in enumerate(order[core]):
            slab = lax.rem(here_ref[0] + away, slabs)
            out_ref[slab * 2 + piece] = sums[:, place * width:(place + 1) * width]


def weighted_sums(replicas, slabs, order, here, parts, blocks):
    part = blocks[0].shape[1] // 2
    total = 2 * sum(b.shape[2] for b in blocks)
    size = replicas * part * total
    return pl.pallas_call(
        functools.partial(combine_kernel, replicas, slabs, order),
        out_shape=jax.ShapeDtypeStruct((replicas, part, total // replicas), jnp.float32),
        in_specs=[pl.BlockSpec(memory_space=pltpu.SMEM)]
        + [pl.BlockSpec(memory_space=VMEM)] * (1 + len(blocks)),
        out_specs=pl.BlockSpec(memory_space=VMEM),
        cost_estimate=pl.CostEstimate(flops=2 * size, bytes_accessed=4 * size, transcendentals=0),
        compiler_params=pltpu.CompilerParams(vmem_limit_bytes=LIMIT),
    )(here.reshape(1), parts, *blocks)


def on_device(activations, out_grads):
    replicas = lax.axis_size("dp")
    slabs = lax.axis_size("tensor")
    here = lax.axis_index("tensor").astype(jnp.int32)
    core = lax.axis_index("dp") % 2
    tokens, slab_rows = activations.shape
    columns = out_grads.shape[1]
    part = columns // replicas
    half = slabs // 2
    rows = slab_rows // 2
    sibling = [(r, r ^ 1) for r in range(replicas)]
    onward = [
        (r * slabs + i, r * slabs + (i + (-1 if r % 2 else 1)) % slabs)
        for r in range(replicas) for i in range(slabs)
    ]

    def own_half(slab):
        return lax.dynamic_slice(slab, (core * rows, 0), (rows, tokens))

    def move(slab):
        return lax.ppermute(slab, ("dp", "tensor"), onward)

    def take(pieces, count):
        taken = []
        while count:
            piece = pieces[0]
            size = min(count, piece.shape[0])
            taken.append(piece[:size])
            count -= size
            pieces = [piece[size:]][: piece.shape[0] > size] + pieces[1:]
        return jnp.concatenate(taken, axis=0), pieces

    mine = activations.T
    chains = [mine, lax.ppermute(mine, "dp", sibling)]
    grads = [out_grads, out_grads]
    chains[1], grads[1] = lax.optimization_barrier((chains[1], grads[1]))
    grads[1] = lax.ppermute(grads[1], "dp", sibling)
    held = [[own_half(slab)] for slab in chains]
    order = [[(0, 0)], [(0, 1)]]
    blocks = []
    gram = jnp.zeros((8, 128), jnp.float32)
    sizes = list(GROUPS)
    for step in range(1, half + 1):
        if step < half:
            chains = [move(slab) for slab in chains]
            if step == 1:
                chains[1], grads[1] = lax.optimization_barrier((chains[1], grads[1]))
            for k in range(2):
                if (step, k) in TIES:
                    place = TIES[step, k]
                    chains[k], blocks[place] = lax.optimization_barrier((chains[k], blocks[place]))
                held[k].append(chains[k])
            order[0] += [(slabs - step, 0), (slabs - step, 1)]
            order[1] += [(step, 0), (step, 1)]
        else:
            for k in range(2):
                held[k].append(move(own_half(chains[k])))
                order[k].append((half, k))
        if sum(piece.shape[0] for piece in held[0]) >= sizes[0]:
            count = sizes.pop(0)
            parts = []
            for k in range(2):
                group, held[k] = take(held[k], count)
                grad = lax.dot_general(
                    grads[k], group, (((0,), (1,)), ((), ())),
                    preferred_element_type=jnp.float32,
                )
                parts.append(grad.reshape(replicas, part, -1))
            ready = jnp.concatenate(parts, axis=1)
            if step < half:
                chains[1], ready = lax.optimization_barrier((chains[1], ready))
            blocks.append(lax.all_to_all(ready, "dp", 0, 0))
    for block in blocks:
        gram = gram_add(replicas, block, gram)
    peers = jnp.broadcast_to(gram, (replicas, *gram.shape))
    parts = sum_and_spread(lax.all_to_all(peers, "dp", 0, 0), slabs)
    parts = lax.all_to_all(parts, "tensor", 0, 0)
    home = weighted_sums(replicas, slabs, order, here, parts, blocks)
    home = lax.all_to_all(home, "dp", 0, 0)
    return home.reshape(columns, -1).T


def solution(mesh):
    return jax.shard_map(
        on_device,
        mesh=mesh,
        in_specs=(P("dp", "tensor"), P("dp", "tensor")),
        out_specs=P("dp", "tensor"),
        check_vma=False,
    )
```

```python
import functools

import jax
import jax.numpy as jnp
from jax import lax
from jax.experimental import pallas as pl
from jax.experimental.pallas import tpu as pltpu
from jax.sharding import PartitionSpec as P

epsilon = 1e-06
GROUP_ENDS = (2, 4, 6, 8)
TIES = {(5, 0): 0, (7, 0): 1}
VMEM = pltpu.VMEM
LIMIT = 48 * 1024 * 1024
EXACT = lax.Precision.HIGHEST


def gram_kernel(replicas, block_ref, before_ref, out_ref):
    part = block_ref.shape[1] // 4
    rows = replicas * part
    i = lax.broadcasted_iota(jnp.int32, (rows, rows), 0)
    j = lax.broadcasted_iota(jnp.int32, (rows, rows), 1)
    whole = jnp.zeros((rows, rows), jnp.float32)
    for core in range(2):
        first = block_ref[:, (3 * core) * part:(3 * core + 1) * part]
        second = block_ref[:, (1 + core) * part:(2 + core) * part]
        both = jnp.concatenate([first, second], axis=1).reshape(rows, -1)
        whole = whole + lax.dot_general(
            both, both, (((1,), (1,)), ((), ())),
            precision=EXACT, preferred_element_type=jnp.float32,
        )
    whole = jnp.where(i % part == j % part, whole, 0.0)
    thin = jnp.sum(whole.reshape(replicas, part, rows), axis=1)
    c = lax.broadcasted_iota(jnp.int32, (rows, 128), 0)
    lane = lax.broadcasted_iota(jnp.int32, (rows, 128), 1)
    total = before_ref[...]
    for k in range(replicas // 8):
        pick = jnp.where(lane == c // part + k * replicas, 1.0, 0.0)
        total = total + jnp.dot(
            thin[k * 8:(k + 1) * 8], pick,
            precision=EXACT, preferred_element_type=jnp.float32,
        )
    out_ref[...] = total


def gram_add(replicas, block, before):
    block = block.reshape(replicas // 2, 2 * block.shape[1], -1)
    size = block.size
    return pl.pallas_call(
        functools.partial(gram_kernel, replicas),
        out_shape=jax.ShapeDtypeStruct((8, 128), jnp.float32),
        in_specs=[pl.BlockSpec(memory_space=VMEM)] * 2,
        out_specs=pl.BlockSpec(memory_space=VMEM),
        cost_estimate=pl.CostEstimate(
            flops=12 * size * replicas * 8, bytes_accessed=4 * size, transcendentals=0
        ),
        compiler_params=pltpu.CompilerParams(vmem_limit_bytes=LIMIT),
    )(block, before)


def spread_kernel(parts_ref, out_ref):
    total = jnp.sum(parts_ref[...], axis=0)
    out_ref[...] = jnp.broadcast_to(total[None], out_ref.shape)


def sum_and_spread(parts, copies):
    return pl.pallas_call(
        spread_kernel,
        out_shape=jax.ShapeDtypeStruct((copies, *parts.shape[1:]), jnp.float32),
        in_specs=[pl.BlockSpec(memory_space=VMEM)],
        out_specs=pl.BlockSpec(memory_space=VMEM),
    )(parts)


def combine_kernel(replicas, slabs, order, counts, here_ref, parts_ref, *refs):
    blocks, out_ref = refs[:-1], refs[-1]
    packed = jnp.sum(parts_ref[...], axis=0)
    gram = jnp.concatenate(
        [packed[:, k * replicas:(k + 1) * replicas] for k in range(replicas // 8)], axis=0
    )
    i = lax.broadcasted_iota(jnp.int32, (replicas, replicas), 0)
    j = lax.broadcasted_iota(jnp.int32, (replicas, replicas), 1)
    down = jnp.ones((replicas, 1), jnp.float32)
    across = jnp.ones((1, replicas), jnp.float32)
    width = 1
    while width < replicas:
        scaled = gram * down * across
        same = i // width == j // width
        partner = i // width == (j // width ^ 1)
        mine = jnp.where(same, scaled, 0.0)
        other = jnp.where(partner, scaled, 0.0)
        own_down = jnp.sum(mine, axis=1, keepdims=True)
        own_across = jnp.sum(mine, axis=0, keepdims=True)
        cross_down = jnp.sum(other, axis=1, keepdims=True)
        cross_across = jnp.sum(other, axis=0, keepdims=True)

        def factor(cross, own, axis):
            cross = jnp.sum(jnp.where(same, cross, 0.0), axis=axis, keepdims=True)
            own = jnp.sum(jnp.where(same, own, 0.0), axis=axis, keepdims=True)
            return 1.0 - cross / (2.0 * (jnp.maximum(own, 0.0) + epsilon))

        new_down = down * factor(cross_across, own_across, 1)
        across = across * factor(cross_down, own_down, 0)
        down = new_down
        width *= 2
    part, width = out_ref.shape[1:]
    for core in range(2):
        place = 0
        for block_ref, count in zip(blocks, counts):
            total = 0.0
            for r in range(replicas):
                row = (r + core) % 2 * part
                total = total + block_ref[r // 2 * 2 + core, row:row + part] * down[r:r + 1]
            for i in range(count):
                away, piece = order[core][place]
                slab = lax.rem(here_ref[0] + away, slabs)
                out_ref[slab * 2 + piece] = total[:, i * width:(i + 1) * width]
                place += 1


def weighted_sums(replicas, slabs, order, counts, width, here, parts, blocks):
    part = blocks[0].shape[1] // 2
    size = sum(b.size for b in blocks)
    return pl.pallas_call(
        functools.partial(combine_kernel, replicas, slabs, order, counts),
        out_shape=jax.ShapeDtypeStruct((replicas, part, width), jnp.float32),
        in_specs=[pl.BlockSpec(memory_space=pltpu.SMEM)]
        + [pl.BlockSpec(memory_space=VMEM)] * (1 + len(blocks)),
        out_specs=pl.BlockSpec(memory_space=VMEM),
        cost_estimate=pl.CostEstimate(flops=2 * size, bytes_accessed=4 * size, transcendentals=0),
        compiler_params=pltpu.CompilerParams(vmem_limit_bytes=LIMIT),
    )(here.reshape(1), parts, *blocks)


def on_device(activations, out_grads):
    replicas = lax.axis_size("dp")
    slabs = lax.axis_size("tensor")
    here = lax.axis_index("tensor").astype(jnp.int32)
    core = lax.axis_index("dp") % 2
    tokens, slab_rows = activations.shape
    columns = out_grads.shape[1]
    part = columns // replicas
    half = slabs // 2
    rows = slab_rows // 2
    sibling = [(r, r ^ 1) for r in range(replicas)]
    onward = [
        (r * slabs + i, r * slabs + (i + (-1 if r % 2 else 1)) % slabs)
        for r in range(replicas) for i in range(slabs)
    ]

    def own_half(slab):
        return lax.dynamic_slice(slab, (core * rows, 0), (rows, tokens))

    def move(slab):
        return lax.ppermute(slab, ("dp", "tensor"), onward)

    mine = activations.T
    chains = [mine, lax.ppermute(mine, "dp", sibling)]
    grads = [out_grads, out_grads]
    chains[1], grads[1] = lax.optimization_barrier((chains[1], grads[1]))
    grads[1] = lax.ppermute(grads[1], "dp", sibling)
    held = [[own_half(slab)] for slab in chains]
    order = [[(0, 0)], [(0, 1)]]
    blocks = []
    gram = jnp.zeros((8, 128), jnp.float32)
    counts = []
    for step in range(1, half + 1):
        if step < half:
            chains = [move(slab) for slab in chains]
            if step == 1:
                chains[1], grads[1] = lax.optimization_barrier((chains[1], grads[1]))
            for k in range(2):
                if (step, k) in TIES:
                    place = TIES[step, k]
                    chains[k], blocks[place] = lax.optimization_barrier((chains[k], blocks[place]))
                held[k].append(chains[k])
            order[0] += [(slabs - step, 0), (slabs - step, 1)]
            order[1] += [(step, 0), (step, 1)]
        else:
            for k in range(2):
                held[k].append(move(own_half(chains[k])))
                order[k].append((half, k))
        if step in GROUP_ENDS:
            size = sum(piece.shape[0] for piece in held[0])
            counts.append(size // rows)
            parts = []
            for k in range(2):
                if size % 128:
                    held[k].append(jnp.zeros((-size % 128, tokens), held[k][0].dtype))
                grad = lax.dot_general(
                    grads[k], jnp.concatenate(held[k], axis=0), (((0,), (1,)), ((), ())),
                    preferred_element_type=jnp.float32,
                )
                parts.append(grad.reshape(replicas, part, -1))
                held[k] = []
            ready = jnp.concatenate(parts, axis=1)
            if step < half:
                chains[1], ready = lax.optimization_barrier((chains[1], ready))
            blocks.append(lax.all_to_all(ready, "dp", 0, 0))
    for block in blocks:
        gram = gram_add(replicas, block, gram)
    peers = jnp.broadcast_to(gram, (replicas, *gram.shape))
    parts = sum_and_spread(lax.all_to_all(peers, "dp", 0, 0), slabs)
    parts = lax.all_to_all(parts, "tensor", 0, 0)
    home = weighted_sums(replicas, slabs, order, counts, rows, here, parts, blocks)
    home = lax.all_to_all(home, "dp", 0, 0)
    return home.reshape(columns, -1).T


def solution(mesh):
    return jax.shard_map(
        on_device,
        mesh=mesh,
        in_specs=(P("dp", "tensor"), P("dp", "tensor")),
        out_specs=P("dp", "tensor"),
        check_vma=False,
    )
```

```python
import functools

import jax
import jax.numpy as jnp
from jax import lax
from jax.experimental import pallas as pl
from jax.experimental.pallas import tpu as pltpu
from jax.sharding import PartitionSpec as P

epsilon = 1e-06
GROUP_ENDS = (2, 4, 6, 8)
TIES = {(5, 0): 0, (7, 0): 1}
VMEM = pltpu.VMEM
LIMIT = 48 * 1024 * 1024
EXACT = lax.Precision.HIGHEST


def gram_kernel(replicas, core_ref, block_ref, before_ref, out_ref):
    part = block_ref.shape[1] // 4
    rows = replicas * part
    i = lax.broadcasted_iota(jnp.int32, (rows, rows), 0)
    j = lax.broadcasted_iota(jnp.int32, (rows, rows), 1)
    whole = jnp.zeros((rows, rows), jnp.float32)
    core = core_ref[0]
    for k in range(2):
        even = pl.multiple_of(core * 2 * part + k * part, part)
        odd = pl.multiple_of((1 - core) * 2 * part + k * part, part)
        both = jnp.concatenate(
            [block_ref[:, pl.ds(even, part)], block_ref[:, pl.ds(odd, part)]], axis=1
        ).reshape(rows, -1)
        whole = whole + lax.dot_general(
            both, both, (((1,), (1,)), ((), ())),
            precision=EXACT, preferred_element_type=jnp.float32,
        )
    whole = jnp.where(i % part == j % part, whole, 0.0)
    thin = jnp.sum(whole.reshape(replicas, part, rows), axis=1)
    c = lax.broadcasted_iota(jnp.int32, (rows, 128), 0)
    lane = lax.broadcasted_iota(jnp.int32, (rows, 128), 1)
    total = before_ref[...]
    for k in range(replicas // 8):
        pick = jnp.where(lane == c // part + k * replicas, 1.0, 0.0)
        total = total + jnp.dot(
            thin[k * 8:(k + 1) * 8], pick,
            precision=EXACT, preferred_element_type=jnp.float32,
        )
    out_ref[...] = total


def gram_add(replicas, core, block, before):
    size = block.size
    return pl.pallas_call(
        functools.partial(gram_kernel, replicas),
        out_shape=jax.ShapeDtypeStruct((8, 128), jnp.float32),
        in_specs=[pl.BlockSpec(memory_space=pltpu.SMEM)] + [pl.BlockSpec(memory_space=VMEM)] * 2,
        out_specs=pl.BlockSpec(memory_space=VMEM),
        cost_estimate=pl.CostEstimate(
            flops=12 * size * replicas * 8, bytes_accessed=4 * size, transcendentals=0
        ),
        compiler_params=pltpu.CompilerParams(vmem_limit_bytes=LIMIT),
    )(core.reshape(1), block, before)


def spread_kernel(parts_ref, out_ref):
    total = jnp.sum(parts_ref[...], axis=0)
    out_ref[...] = jnp.broadcast_to(total[None], out_ref.shape)


def sum_and_spread(parts, copies):
    return pl.pallas_call(
        spread_kernel,
        out_shape=jax.ShapeDtypeStruct((copies, *parts.shape[1:]), jnp.float32),
        in_specs=[pl.BlockSpec(memory_space=VMEM)],
        out_specs=pl.BlockSpec(memory_space=VMEM),
    )(parts)


def combine_kernel(replicas, slabs, order, counts, here_ref, core_ref, parts_ref, *refs):
    blocks, out_ref = refs[:-1], refs[-1]
    packed = jnp.sum(parts_ref[...], axis=0)
    gram = jnp.concatenate(
        [packed[:, k * replicas:(k + 1) * replicas] for k in range(replicas // 8)], axis=0
    )
    i = lax.broadcasted_iota(jnp.int32, (replicas, replicas), 0)
    j = lax.broadcasted_iota(jnp.int32, (replicas, replicas), 1)
    down = jnp.ones((replicas, 1), jnp.float32)
    across = jnp.ones((1, replicas), jnp.float32)
    width = 1
    while width < replicas:
        scaled = gram * down * across
        same = i // width == j // width
        partner = i // width == (j // width ^ 1)
        mine = jnp.where(same, scaled, 0.0)
        other = jnp.where(partner, scaled, 0.0)
        own_down = jnp.sum(mine, axis=1, keepdims=True)
        own_across = jnp.sum(mine, axis=0, keepdims=True)
        cross_down = jnp.sum(other, axis=1, keepdims=True)
        cross_across = jnp.sum(other, axis=0, keepdims=True)

        def factor(cross, own, axis):
            cross = jnp.sum(jnp.where(same, cross, 0.0), axis=axis, keepdims=True)
            own = jnp.sum(jnp.where(same, own, 0.0), axis=axis, keepdims=True)
            return 1.0 - cross / (2.0 * (jnp.maximum(own, 0.0) + epsilon))

        new_down = down * factor(cross_across, own_across, 1)
        across = across * factor(cross_down, own_down, 0)
        down = new_down
        width *= 2
    part, width = out_ref.shape[1:]
    here, core = here_ref[0], core_ref[0]
    starts = [pl.multiple_of(core * part, part), pl.multiple_of((1 - core) * part, part)]
    out_ref[...] = jnp.zeros(out_ref.shape, jnp.float32)
    place = 0
    for block_ref, count in zip(blocks, counts):
        total = 0.0
        for r in range(replicas):
            total = total + block_ref[r // 2, pl.ds(starts[r % 2], part)] * down[r:r + 1]
        for i in range(count):
            step, piece = order[place]
            away = jnp.where(core == 0, slabs - step, step)
            slab = lax.rem(here + away, slabs)
            piece = core if piece is None else piece
            out_ref[slab * 2 + piece] = total[:, i * width:(i + 1) * width]
            place += 1


def weighted_sums(replicas, slabs, order, counts, width, here, core, parts, blocks):
    part = blocks[0].shape[1] // 2
    size = sum(b.size for b in blocks)
    return pl.pallas_call(
        functools.partial(combine_kernel, replicas, slabs, order, counts),
        out_shape=jax.ShapeDtypeStruct((replicas, part, width), jnp.float32),
        in_specs=[pl.BlockSpec(memory_space=pltpu.SMEM)] * 2
        + [pl.BlockSpec(memory_space=VMEM)] * (1 + len(blocks)),
        out_specs=pl.BlockSpec(memory_space=VMEM),
        cost_estimate=pl.CostEstimate(flops=2 * size, bytes_accessed=4 * size, transcendentals=0),
        compiler_params=pltpu.CompilerParams(vmem_limit_bytes=LIMIT),
    )(here.reshape(1), core.reshape(1), parts, *blocks)


def on_device(activations, out_grads):
    replicas = lax.axis_size("dp")
    slabs = lax.axis_size("tensor")
    here = lax.axis_index("tensor").astype(jnp.int32)
    core = lax.axis_index("dp").astype(jnp.int32) % 2
    tokens, slab_rows = activations.shape
    columns = out_grads.shape[1]
    chips = replicas // 2
    same_core = [list(range(k, replicas, 2)) for k in range(2)]
    half = slabs // 2
    rows = slab_rows // 2
    sibling = [(r, r ^ 1) for r in range(replicas)]
    onward = [
        (r * slabs + i, r * slabs + (i + (-1 if r % 2 else 1)) % slabs)
        for r in range(replicas) for i in range(slabs)
    ]

    def own_half(slab):
        return lax.dynamic_slice(slab, (core * rows, 0), (rows, tokens))

    def move(slab):
        return lax.ppermute(slab, ("dp", "tensor"), onward)

    mine = activations.T
    chains = [mine, lax.ppermute(mine, "dp", sibling)]
    grads = [out_grads, out_grads]
    chains[1], grads[1] = lax.optimization_barrier((chains[1], grads[1]))
    grads[1] = lax.ppermute(grads[1], "dp", sibling)
    held = [[own_half(slab)] for slab in chains]
    order = [(0, None)]
    blocks = []
    gram = jnp.zeros((8, 128), jnp.float32)
    counts = []
    for step in range(1, half + 1):
        if step < half:
            chains = [move(slab) for slab in chains]
            if step == 1:
                chains[1], grads[1] = lax.optimization_barrier((chains[1], grads[1]))
            for k in range(2):
                if (step, k) in TIES:
                    place = TIES[step, k]
                    chains[k], blocks[place] = lax.optimization_barrier((chains[k], blocks[place]))
                held[k].append(chains[k])
            order += [(step, 0), (step, 1)]
        else:
            for k in range(2):
                held[k].append(move(own_half(chains[k])))
            order.append((half, None))
        if step in GROUP_ENDS:
            size = sum(piece.shape[0] for piece in held[0])
            counts.append(size // rows)
            parts = []
            for k in range(2):
                if size % 128:
                    held[k].append(jnp.zeros((-size % 128, tokens), held[k][0].dtype))
                grad = lax.dot_general(
                    grads[k], jnp.concatenate(held[k], axis=0), (((0,), (1,)), ((), ())),
                    preferred_element_type=jnp.float32,
                )
                parts.append(grad.reshape(chips, columns // chips, -1))
                held[k] = []
            ready = jnp.concatenate(parts, axis=1)
            if step < half:
                chains[1], ready = lax.optimization_barrier((chains[1], ready))
            blocks.append(lax.all_to_all(ready, "dp", 0, 0, axis_index_groups=same_core))
    for block in blocks:
        gram = gram_add(replicas, core, block, gram)
    peers = jnp.broadcast_to(gram, (replicas, *gram.shape))
    parts = sum_and_spread(lax.all_to_all(peers, "dp", 0, 0), slabs)
    parts = lax.all_to_all(parts, "tensor", 0, 0)
    home = weighted_sums(replicas, slabs, order, counts, rows, here, core, parts, blocks)
    home = lax.all_to_all(home, "dp", 0, 0)
    home = jnp.sum(home.reshape(chips, 2, columns // chips, -1), axis=1)
    return home.reshape(columns, -1).T


def solution(mesh):
    return jax.shard_map(
        on_device,
        mesh=mesh,
        in_specs=(P("dp", "tensor"), P("dp", "tensor")),
        out_specs=P("dp", "tensor"),
        check_vma=False,
    )
```

```python
import functools

import jax
import jax.numpy as jnp
from jax import lax
from jax.experimental import pallas as pl
from jax.experimental.pallas import tpu as pltpu
from jax.sharding import PartitionSpec as P

epsilon = 1e-06
GROUP_ENDS = (2, 4, 6, 8)
TIES = {(5, 0): 0, (6, 1): 1}
VMEM = pltpu.VMEM
LIMIT = 48 * 1024 * 1024
EXACT = lax.Precision.HIGHEST


def gram_kernel(replicas, core_ref, block_ref, before_ref, out_ref):
    part = block_ref.shape[1] // 4
    rows = replicas * part
    i = lax.broadcasted_iota(jnp.int32, (rows, rows), 0)
    j = lax.broadcasted_iota(jnp.int32, (rows, rows), 1)
    whole = jnp.zeros((rows, rows), jnp.float32)
    core = core_ref[0]
    for k in range(2):
        even = pl.multiple_of(core * 2 * part + k * part, part)
        odd = pl.multiple_of((1 - core) * 2 * part + k * part, part)
        both = jnp.concatenate(
            [block_ref[:, pl.ds(even, part)], block_ref[:, pl.ds(odd, part)]], axis=1
        ).reshape(rows, -1)
        whole = whole + lax.dot_general(
            both, both, (((1,), (1,)), ((), ())),
            precision=EXACT, preferred_element_type=jnp.float32,
        )
    whole = jnp.where(i % part == j % part, whole, 0.0)
    thin = jnp.sum(whole.reshape(replicas, part, rows), axis=1)
    c = lax.broadcasted_iota(jnp.int32, (rows, 128), 0)
    lane = lax.broadcasted_iota(jnp.int32, (rows, 128), 1)
    total = before_ref[...]
    for k in range(replicas // 8):
        pick = jnp.where(lane == c // part + k * replicas, 1.0, 0.0)
        total = total + jnp.dot(
            thin[k * 8:(k + 1) * 8], pick,
            precision=EXACT, preferred_element_type=jnp.float32,
        )
    out_ref[...] = total


def gram_add(replicas, core, block, before):
    size = block.size
    return pl.pallas_call(
        functools.partial(gram_kernel, replicas),
        out_shape=jax.ShapeDtypeStruct((8, 128), jnp.float32),
        in_specs=[pl.BlockSpec(memory_space=pltpu.SMEM)] + [pl.BlockSpec(memory_space=VMEM)] * 2,
        out_specs=pl.BlockSpec(memory_space=VMEM),
        cost_estimate=pl.CostEstimate(
            flops=12 * size * replicas * 8, bytes_accessed=4 * size, transcendentals=0
        ),
        compiler_params=pltpu.CompilerParams(vmem_limit_bytes=LIMIT),
    )(core.reshape(1), block, before)


def spread_kernel(parts_ref, out_ref):
    total = jnp.sum(parts_ref[...], axis=0)
    out_ref[...] = jnp.broadcast_to(total[None], out_ref.shape)


def sum_and_spread(parts, copies):
    return pl.pallas_call(
        spread_kernel,
        out_shape=jax.ShapeDtypeStruct((copies, *parts.shape[1:]), jnp.float32),
        in_specs=[pl.BlockSpec(memory_space=VMEM)],
        out_specs=pl.BlockSpec(memory_space=VMEM),
    )(parts)


def combine_kernel(replicas, slabs, order, counts, here_ref, core_ref, parts_ref, *refs):
    blocks, out_ref = refs[:-1], refs[-1]
    packed = jnp.sum(parts_ref[...], axis=0)
    gram = jnp.concatenate(
        [packed[:, k * replicas:(k + 1) * replicas] for k in range(replicas // 8)], axis=0
    )
    i = lax.broadcasted_iota(jnp.int32, (replicas, replicas), 0)
    j = lax.broadcasted_iota(jnp.int32, (replicas, replicas), 1)
    down = jnp.ones((replicas, 1), jnp.float32)
    across = jnp.ones((1, replicas), jnp.float32)
    width = 1
    while width < replicas:
        scaled = gram * down * across
        same = i // width == j // width
        partner = i // width == (j // width ^ 1)
        mine = jnp.where(same, scaled, 0.0)
        other = jnp.where(partner, scaled, 0.0)
        own_down = jnp.sum(mine, axis=1, keepdims=True)
        own_across = jnp.sum(mine, axis=0, keepdims=True)
        cross_down = jnp.sum(other, axis=1, keepdims=True)
        cross_across = jnp.sum(other, axis=0, keepdims=True)

        def factor(cross, own, axis):
            cross = jnp.sum(jnp.where(same, cross, 0.0), axis=axis, keepdims=True)
            own = jnp.sum(jnp.where(same, own, 0.0), axis=axis, keepdims=True)
            return 1.0 - cross / (2.0 * (jnp.maximum(own, 0.0) + epsilon))

        new_down = down * factor(cross_across, own_across, 1)
        across = across * factor(cross_down, own_down, 0)
        down = new_down
        width *= 2
    part, width = out_ref.shape[1:]
    here, core = here_ref[0], core_ref[0]
    starts = [pl.multiple_of(core * part, part), pl.multiple_of((1 - core) * part, part)]
    out_ref[...] = jnp.zeros(out_ref.shape, jnp.float32)
    place = 0
    for block_ref, count in zip(blocks, counts):
        total = 0.0
        for r in range(replicas):
            total = total + block_ref[r // 2, pl.ds(starts[r % 2], part)] * down[r:r + 1]
        for i in range(count):
            step, piece = order[place]
            away = jnp.where(core == 0, slabs - step, step)
            slab = lax.rem(here + away, slabs)
            piece = core if piece is None else piece
            out_ref[slab * 2 + piece] = total[:, i * width:(i + 1) * width]
            place += 1


def weighted_sums(replicas, slabs, order, counts, width, here, core, parts, blocks):
    part = blocks[0].shape[1] // 2
    size = sum(b.size for b in blocks)
    return pl.pallas_call(
        functools.partial(combine_kernel, replicas, slabs, order, counts),
        out_shape=jax.ShapeDtypeStruct((replicas, part, width), jnp.float32),
        in_specs=[pl.BlockSpec(memory_space=pltpu.SMEM)] * 2
        + [pl.BlockSpec(memory_space=VMEM)] * (1 + len(blocks)),
        out_specs=pl.BlockSpec(memory_space=VMEM),
        cost_estimate=pl.CostEstimate(flops=2 * size, bytes_accessed=4 * size, transcendentals=0),
        compiler_params=pltpu.CompilerParams(vmem_limit_bytes=LIMIT),
    )(here.reshape(1), core.reshape(1), parts, *blocks)


def on_device(activations, out_grads):
    replicas = lax.axis_size("dp")
    slabs = lax.axis_size("tensor")
    here = lax.axis_index("tensor").astype(jnp.int32)
    core = lax.axis_index("dp").astype(jnp.int32) % 2
    tokens, slab_rows = activations.shape
    columns = out_grads.shape[1]
    chips = replicas // 2
    same_core = [list(range(k, replicas, 2)) for k in range(2)]
    half = slabs // 2
    rows = slab_rows // 2
    sibling = [(r, r ^ 1) for r in range(replicas)]
    onward = [
        (r * slabs + i, r * slabs + (i + (-1 if r % 2 else 1)) % slabs)
        for r in range(replicas) for i in range(slabs)
    ]

    def own_half(slab):
        return lax.dynamic_slice(slab, (core * rows, 0), (rows, tokens))

    def move(slab):
        return lax.ppermute(slab, ("dp", "tensor"), onward)

    mine = activations.T
    chains = [mine, lax.ppermute(mine, "dp", sibling)]
    grads = [out_grads, out_grads]
    chains[1], grads[1] = lax.optimization_barrier((chains[1], grads[1]))
    grads[1] = lax.ppermute(grads[1], "dp", sibling)
    held = [[own_half(slab)] for slab in chains]
    order = [(0, None)]
    blocks = []
    gram = jnp.zeros((8, 128), jnp.float32)
    counts = []
    for step in range(1, half + 1):
        if step < half:
            chains = [move(slab) for slab in chains]
            if step == 1:
                chains[1], grads[1] = lax.optimization_barrier((chains[1], grads[1]))
            for k in range(2):
                if (step, k) in TIES:
                    place = TIES[step, k]
                    chains[k], blocks[place] = lax.optimization_barrier((chains[k], blocks[place]))
                held[k].append(chains[k])
            order += [(step, 0), (step, 1)]
        else:
            for k in range(2):
                held[k].append(move(own_half(chains[k])))
            order.append((half, None))
        if step in GROUP_ENDS:
            size = sum(piece.shape[0] for piece in held[0])
            counts.append(size // rows)
            parts = []
            for k in range(2):
                if size % 128:
                    held[k].append(jnp.zeros((-size % 128, tokens), held[k][0].dtype))
                grad = lax.dot_general(
                    grads[k], jnp.concatenate(held[k], axis=0), (((0,), (1,)), ((), ())),
                    preferred_element_type=jnp.float32,
                )
                parts.append(grad.reshape(chips, columns // chips, -1))
                held[k] = []
            ready = jnp.concatenate(parts, axis=1)
            if step < half:
                chains[1], ready = lax.optimization_barrier((chains[1], ready))
            blocks.append(lax.all_to_all(ready, "dp", 0, 0, axis_index_groups=same_core))
    for block in blocks:
        gram = gram_add(replicas, core, block, gram)
    peers = jnp.broadcast_to(gram, (replicas, *gram.shape))
    parts = sum_and_spread(lax.all_to_all(peers, "dp", 0, 0), slabs)
    parts = lax.all_to_all(parts, "tensor", 0, 0)
    home = weighted_sums(replicas, slabs, order, counts, rows, here, core, parts, blocks)
    home = lax.all_to_all(home, "dp", 0, 0)
    home = jnp.sum(home.reshape(chips, 2, columns // chips, -1), axis=1)
    return home.reshape(columns, -1).T


def solution(mesh):
    return jax.shard_map(
        on_device,
        mesh=mesh,
        in_specs=(P("dp", "tensor"), P("dp", "tensor")),
        out_specs=P("dp", "tensor"),
        check_vma=False,
    )
```

```python
import functools

import jax
import jax.numpy as jnp
from jax import lax
from jax.experimental import pallas as pl
from jax.experimental.pallas import tpu as pltpu
from jax.sharding import PartitionSpec as P

epsilon = 1e-06
GROUP_ENDS = (2, 4, 6, 8)
TIES = {(5, 0): 0, (6, 1): 1}
VMEM = pltpu.VMEM
LIMIT = 48 * 1024 * 1024
EXACT = lax.Precision.HIGHEST


def gram_kernel(replicas, core_ref, block_ref, before_ref, out_ref):
    part = block_ref.shape[1] // 4
    rows = replicas * part
    i = lax.broadcasted_iota(jnp.int32, (rows, rows), 0)
    j = lax.broadcasted_iota(jnp.int32, (rows, rows), 1)
    whole = jnp.zeros((rows, rows), jnp.float32)
    core = core_ref[0]
    for k in range(2):
        even = pl.multiple_of(core * 2 * part + k * part, part)
        odd = pl.multiple_of((1 - core) * 2 * part + k * part, part)
        both = jnp.concatenate(
            [block_ref[:, pl.ds(even, part)], block_ref[:, pl.ds(odd, part)]], axis=1
        ).reshape(rows, -1)
        whole = whole + lax.dot_general(
            both, both, (((1,), (1,)), ((), ())),
            precision=EXACT, preferred_element_type=jnp.float32,
        )
    whole = jnp.where(i % part == j % part, whole, 0.0)
    thin = jnp.sum(whole.reshape(replicas, part, rows), axis=1)
    c = lax.broadcasted_iota(jnp.int32, (rows, 128), 0)
    lane = lax.broadcasted_iota(jnp.int32, (rows, 128), 1)
    total = before_ref[...]
    for k in range(replicas // 8):
        pick = jnp.where(lane == c // part + k * replicas, 1.0, 0.0)
        total = total + jnp.dot(
            thin[k * 8:(k + 1) * 8], pick,
            precision=EXACT, preferred_element_type=jnp.float32,
        )
    out_ref[...] = total


def gram_add(replicas, core, block, before):
    size = block.size
    return pl.pallas_call(
        functools.partial(gram_kernel, replicas),
        out_shape=jax.ShapeDtypeStruct((8, 128), jnp.float32),
        in_specs=[pl.BlockSpec(memory_space=pltpu.SMEM)] + [pl.BlockSpec(memory_space=VMEM)] * 2,
        out_specs=pl.BlockSpec(memory_space=VMEM),
        cost_estimate=pl.CostEstimate(
            flops=12 * size * replicas * 8, bytes_accessed=4 * size, transcendentals=0
        ),
        compiler_params=pltpu.CompilerParams(vmem_limit_bytes=LIMIT),
    )(core.reshape(1), block, before)


def spread_kernel(parts_ref, out_ref):
    total = jnp.sum(parts_ref[...], axis=0)
    out_ref[...] = jnp.broadcast_to(total[None], out_ref.shape)


def sum_and_spread(parts, copies):
    return pl.pallas_call(
        spread_kernel,
        out_shape=jax.ShapeDtypeStruct((copies, *parts.shape[1:]), jnp.float32),
        in_specs=[pl.BlockSpec(memory_space=VMEM)],
        out_specs=pl.BlockSpec(memory_space=VMEM),
    )(parts)


def combine_kernel(replicas, slabs, layouts, here_ref, core_ref, parts_ref, *refs):
    blocks, out_ref = refs[:-1], refs[-1]
    packed = jnp.sum(parts_ref[...], axis=0)
    gram = jnp.concatenate(
        [packed[:, k * replicas:(k + 1) * replicas] for k in range(replicas // 8)], axis=0
    )
    i = lax.broadcasted_iota(jnp.int32, (replicas, replicas), 0)
    j = lax.broadcasted_iota(jnp.int32, (replicas, replicas), 1)
    down = jnp.ones((replicas, 1), jnp.float32)
    across = jnp.ones((1, replicas), jnp.float32)
    width = 1
    while width < replicas:
        scaled = gram * down * across
        same = i // width == j // width
        partner = i // width == (j // width ^ 1)
        mine = jnp.where(same, scaled, 0.0)
        other = jnp.where(partner, scaled, 0.0)
        own_down = jnp.sum(mine, axis=1, keepdims=True)
        own_across = jnp.sum(mine, axis=0, keepdims=True)
        cross_down = jnp.sum(other, axis=1, keepdims=True)
        cross_across = jnp.sum(other, axis=0, keepdims=True)

        def factor(cross, own, axis):
            cross = jnp.sum(jnp.where(same, cross, 0.0), axis=axis, keepdims=True)
            own = jnp.sum(jnp.where(same, own, 0.0), axis=axis, keepdims=True)
            return 1.0 - cross / (2.0 * (jnp.maximum(own, 0.0) + epsilon))

        new_down = down * factor(cross_across, own_across, 1)
        across = across * factor(cross_down, own_down, 0)
        down = new_down
        width *= 2
    part, width = out_ref.shape[1:]
    here, core = here_ref[0], core_ref[0]
    starts = [pl.multiple_of(core * part, part), pl.multiple_of((1 - core) * part, part)]
    out_ref[...] = jnp.zeros(out_ref.shape, jnp.float32)
    for block_ref, layout in zip(blocks, layouts):
        total = 0.0
        for r in range(replicas):
            total = total + block_ref[r // 2, pl.ds(starts[r % 2], part)] * down[r:r + 1]
        for step, piece, place, count, column in layout:
            away = jnp.where(core == 0, slabs - step, step)
            slab = lax.rem(here + away, slabs)
            piece = core if piece is None else piece
            out_ref[slab * 2 + piece, :, place:place + count] = total[:, column:column + count]


def weighted_sums(replicas, slabs, layouts, width, here, core, parts, blocks):
    part = blocks[0].shape[1] // 2
    size = sum(b.size for b in blocks)
    return pl.pallas_call(
        functools.partial(combine_kernel, replicas, slabs, layouts),
        out_shape=jax.ShapeDtypeStruct((replicas, part, width), jnp.float32),
        in_specs=[pl.BlockSpec(memory_space=pltpu.SMEM)] * 2
        + [pl.BlockSpec(memory_space=VMEM)] * (1 + len(blocks)),
        out_specs=pl.BlockSpec(memory_space=VMEM),
        cost_estimate=pl.CostEstimate(flops=2 * size, bytes_accessed=4 * size, transcendentals=0),
        compiler_params=pltpu.CompilerParams(vmem_limit_bytes=LIMIT),
    )(here.reshape(1), core.reshape(1), parts, *blocks)


def on_device(activations, out_grads):
    replicas = lax.axis_size("dp")
    slabs = lax.axis_size("tensor")
    here = lax.axis_index("tensor").astype(jnp.int32)
    core = lax.axis_index("dp").astype(jnp.int32) % 2
    tokens, slab_rows = activations.shape
    columns = out_grads.shape[1]
    chips = replicas // 2
    same_core = [list(range(k, replicas, 2)) for k in range(2)]
    half = slabs // 2
    rows = slab_rows // 2
    sibling = [(r, r ^ 1) for r in range(replicas)]
    onward = [
        (r * slabs + i, r * slabs + (i + (-1 if r % 2 else 1)) % slabs)
        for r in range(replicas) for i in range(slabs)
    ]

    def own_half(slab):
        return lax.dynamic_slice(slab, (core * rows, 0), (rows, tokens))

    def move(slab):
        return lax.ppermute(slab, ("dp", "tensor"), onward)

    mine = activations.T
    chains = [mine, lax.ppermute(mine, "dp", sibling)]
    grads = [out_grads, out_grads]
    chains[1], grads[1] = lax.optimization_barrier((chains[1], grads[1]))
    grads[1] = lax.ppermute(grads[1], "dp", sibling)
    def layout_of(order):
        layout, column = [], 0
        for step, start, count in order:
            while count:
                piece = None if start is None else start // rows
                place = 0 if start is None else start % rows
                run = min(count, rows - place)
                layout.append((step, piece, place, run, column))
                column, count = column + run, count - run
                start = None if start is None else start + run
        return layout

    held = [[own_half(slab)] for slab in chains]
    order = [(0, None, rows)]
    left, left_order = [[], []], []
    blocks, layouts = [], []
    gram = jnp.zeros((8, 128), jnp.float32)
    for step in range(1, half + 1):
        if step < half:
            chains = [move(slab) for slab in chains]
            if step == 1:
                chains[1], grads[1] = lax.optimization_barrier((chains[1], grads[1]))
            for k in range(2):
                if (step, k) in TIES:
                    place = TIES[step, k]
                    chains[k], blocks[place] = lax.optimization_barrier((chains[k], blocks[place]))
                held[k].append(chains[k])
            order.append((step, 0, slab_rows))
        else:
            for k in range(2):
                held[k].append(move(own_half(chains[k])))
            order.append((half, None, rows))
        if step in GROUP_ENDS:
            if step < half:
                spare = sum(piece.shape[0] for piece in held[0]) % 128
                if spare:
                    for k in range(2):
                        left[k].append(held[k][-1][-spare:])
                        held[k][-1] = held[k][-1][:-spare]
                    last, start, count = order.pop()
                    order.append((last, start, count - spare))
                    left_order.append((last, start + count - spare, spare))
            else:
                held = [held[k] + left[k] for k in range(2)]
                order += left_order
            layouts.append(layout_of(order))
            order, parts = [], []
            for k in range(2):
                size = sum(piece.shape[0] for piece in held[k])
                if size % 128:
                    held[k].append(jnp.zeros((-size % 128, tokens), held[k][0].dtype))
                grad = lax.dot_general(
                    grads[k], jnp.concatenate(held[k], axis=0), (((0,), (1,)), ((), ())),
                    preferred_element_type=jnp.float32,
                )
                parts.append(grad.reshape(chips, columns // chips, -1))
                held[k] = []
            ready = jnp.concatenate(parts, axis=1)
            if step < half:
                chains[1], ready = lax.optimization_barrier((chains[1], ready))
            blocks.append(lax.all_to_all(ready, "dp", 0, 0, axis_index_groups=same_core))
    for block in blocks:
        gram = gram_add(replicas, core, block, gram)
    peers = jnp.broadcast_to(gram, (replicas, *gram.shape))
    parts = sum_and_spread(lax.all_to_all(peers, "dp", 0, 0), slabs)
    parts = lax.all_to_all(parts, "tensor", 0, 0)
    home = weighted_sums(replicas, slabs, layouts, rows, here, core, parts, blocks)
    home = lax.all_to_all(home, "dp", 0, 0)
    home = jnp.sum(home.reshape(chips, 2, columns // chips, -1), axis=1)
    return home.reshape(columns, -1).T


def solution(mesh):
    return jax.shard_map(
        on_device,
        mesh=mesh,
        in_specs=(P("dp", "tensor"), P("dp", "tensor")),
        out_specs=P("dp", "tensor"),
        check_vma=False,
    )
```
